32 devices in a mesh: ctx: 8 (over y, x, core), row: 4 (over z).
Axes of the slice: x: 2, y: 2, z: 4, core: 2. Of those that a mesh axis runs over, the one named last changes fastest.
Arguments:
- latent_cache: bfloat16 [32768, 576], P(('ctx', 'row')), may hold values from -8 to 8
- index_keys: bfloat16 [32768, 128], P('ctx'), may hold values from -6 to 6
- query_latent: bfloat16 [128, 128, 576], P(('row', 'ctx')), may hold values from -100 to 99
- index_query: bfloat16 [128, 64, 128], P(('row', 'ctx')), may hold values from -0.5 to 0.5
- index_gates: bfloat16 [128, 64], P(('row', 'ctx')), may hold values from -0.75 to 0.75
- selected: int32 [128, 2048], P(('row', 'ctx')), may hold values from 0 to 32767, as said below
Outputs:
- attended: bfloat16 [128, 128, 512], P(('row', 'ctx'))
- index_scores: float32 [128, 32768], P('row', 'ctx')
The draws below stay inside these ranges and needn't reach their ends.
Inputs may be any that keep to these rules, and one draw needn't show every extreme that they name: `selected`: each row names 2048 different tokens. Among the tokens of one index of ctx (s * 4096 <= t < (s + 1) * 4096) a row names at most 256, and exactly 256 in one such range; a row names at most one token in each aligned run of 16 tokens.
All inputs are finite; a program needn't handle non-finite values.
Results may differ from the reference program's by a relative error of at most 0.0045.
Values may be sent and summed in bfloat16 or wider, within the bound.
No kernel may reach another device: no remote copies, remote signals or barrier semaphores. Data moves between devices by JAX's collectives and lax.ppermute only.
A program may use at most 256 MiB of HBM per device.

```python
import jax
import jax.numpy as jnp
from jax import lax

HEADS = 128
LATENT = 512
ROPE = 64
IHEADS = 64
IDIM = 128
TOPK = 2048
SCORE_DIM = 192
SEL_MOST = 256
TOK_DEV = 4096
CACHE = 32768
ROWS = 128


def pick_tokens(key):
    base = jax.random.fold_in(key, 11)
    key_bias, key_forced, key_noise, key_jitter = jax.random.split(base, 4)
    shards = CACHE // TOK_DEV
    slots = shards * SEL_MOST
    spacing = TOK_DEV // SEL_MOST
    bias = jax.random.randint(key_bias, (ROWS, shards), 0, shards) + jnp.arange(shards, dtype=jnp.int32)[None, :]
    forced = jax.random.randint(key_forced, (ROWS,), 0, shards)
    bias = jnp.where(jnp.arange(shards, dtype=jnp.int32)[None, :] == forced[:, None], 8 * shards, bias)
    shard_of_slot = jnp.arange(slots, dtype=jnp.int32) // SEL_MOST
    noise = jax.random.randint(key_noise, (ROWS, slots), 0, 2 * shards)
    ranking = (bias[:, shard_of_slot] + noise) * slots + jnp.arange(slots, dtype=jnp.int32)[None, :]
    chosen = lax.top_k(ranking, TOPK)[1].astype(jnp.int32)
    shard = chosen // SEL_MOST
    place = chosen % SEL_MOST
    jitter = jax.random.randint(key_jitter, (ROWS, TOPK), 0, spacing)
    return (shard * TOK_DEV + place * spacing + jitter).astype(jnp.int32)


def cache_field(key):
    base = jax.random.normal(jax.random.fold_in(key, 23), (CACHE, LATENT + ROPE), jnp.float32)
    base = jnp.clip(base, -6.0, 6.0)
    return base


def draw_latent_cache(key, part):
    return cache_field(key).astype(jnp.bfloat16)


def draw_selected(key, part):
    return pick_tokens(key)


def draw_query_latent(key, part):
    query = jnp.clip(jax.random.normal(jax.random.fold_in(key, 37), (ROWS, HEADS, LATENT + ROPE), jnp.float32), -6.0, 6.0)
    return query.astype(jnp.bfloat16)


def block_scale(own_key, shape, pieces, least, high):
    loudness = 1.0
    for axis_at, parts in pieces:
        steps = jax.random.uniform(jax.random.fold_in(jax.random.fold_in(own_key, 6), axis_at), (parts,), jnp.float32, least / len(pieces), high / len(pieces))
        loudness = loudness * jnp.repeat(jnp.exp(steps), shape[axis_at] // parts).reshape((-1,) + (1,) * (len(shape) - 1 - axis_at))
    return loudness


def gaussian(key, shape, spread, limit, cuts=(), kind=jnp.bfloat16):
    entries = jax.random.normal(key, shape, jnp.float32) * spread
    if len(cuts) > 0:
        entries = block_scale(key, shape, cuts, -0.22, 0.18) * entries
    return jnp.clip(entries, min=-limit, max=limit).astype(kind)


def setup_inputs(seed: int = 0) -> dict:
    key_list = jax.random.split(jax.random.key(seed), 7)
    latent_cache = draw_latent_cache(jax.random.fold_in(key_list[6], 71), 0)
    index_keys = gaussian(key_list[1], (CACHE, IDIM), 1.0, 6.0, ((0, 8),))
    query_latent = draw_query_latent(jax.random.fold_in(key_list[6], 71), 0)
    index_query = gaussian(key_list[3], (ROWS, IHEADS, IDIM), IDIM ** -0.5, 0.5, ((0, 32),))
    index_gates = gaussian(key_list[4], (ROWS, IHEADS), IHEADS ** -0.5, 0.75, ((0, 32),))
    selected = draw_selected(jax.random.fold_in(key_list[6], 71), 0)
    return {"latent_cache": latent_cache, "index_keys": index_keys, "query_latent": query_latent, "index_query": index_query, "index_gates": index_gates, "selected": selected}


def reference(latent_cache, index_keys, query_latent, index_query, index_gates, selected):
    scale = SCORE_DIM ** -0.5

    def attend_row(pair):
        query, picks = pair
        keys = latent_cache[picks]
        scores = jnp.dot(query, keys.T, preferred_element_type=jnp.float32) * scale
        peak = jnp.max(scores, axis=1, keepdims=True)
        weights = jnp.exp(scores - peak).astype(jnp.bfloat16)
        totals = jnp.sum(weights.astype(jnp.float32), axis=1)
        sums = jnp.dot(weights, keys[:, :LATENT], preferred_element_type=jnp.float32)
        return (sums / totals[:, None]).astype(jnp.bfloat16)

    attended = lax.map(attend_row, (query_latent, selected))

    def index_row(pair):
        iquery, gates = pair
        logits = jnp.dot(iquery, index_keys.T, preferred_element_type=jnp.float32)
        return jnp.sum(gates.astype(jnp.float32)[:, None] * jnp.maximum(logits, 0.0), axis=0)

    index_scores = lax.map(index_row, (index_query, index_gates))
    return attended, index_scores
```

```python
import functools

import jax
import jax.numpy as jnp
from jax import lax
from jax.experimental import pallas as pl
from jax.experimental.pallas import tpu as pltpu
from jax.sharding import PartitionSpec as P

LATENT = 512
SCORE_DIM = 192
SEL_MOST = 256
TOK_DEV = 4096
RUN = TOK_DEV // SEL_MOST
LANES = 128
AUX = 16
SCALE = SCORE_DIM ** (-0.5) * 1.4426950408889634
VMEM = pltpu.VMEM


def whole_vmem(count):
    return [pl.BlockSpec(memory_space=VMEM)] * count


def params():
    return pltpu.CompilerParams(vmem_limit_bytes=56 * 1024 * 1024)


def table_kernel(query_ref, selected_ref, out_ref):
    rows, width, _ = query_ref.shape
    his = out_ref.shape[1] - width
    picks = selected_ref.shape[1]
    hi_at = lax.broadcasted_iota(jnp.int32, (his, picks), 0)
    lo_at = lax.broadcasted_iota(jnp.int32, (LANES, picks), 0)
    out_ref[:, :width, :] = query_ref[...]
    for row in range(rows):
        token = selected_ref[row : row + 1, :]
        offset = (token % RUN + 1).astype(jnp.float32)
        run = token // RUN
        high = (hi_at == run // LANES).astype(jnp.float32).astype(jnp.bfloat16)
        low = jnp.where(lo_at == run % LANES, offset, 0.0).astype(jnp.bfloat16)
        table = lax.dot_general(
            high, low, (((1,), (1,)), ((), ())), preferred_element_type=jnp.float32
        )
        out_ref[row, width:, :] = table.astype(jnp.bfloat16)


def with_table(query, selected, his):
    rows, width, heads = query.shape
    return pl.pallas_call(
        table_kernel,
        out_shape=jax.ShapeDtypeStruct((rows, width + his, heads), jnp.bfloat16),
        in_specs=whole_vmem(2),
        out_specs=pl.BlockSpec(memory_space=VMEM),
        compiler_params=params(),
        name="table",
    )(query, selected)


def three(value):
    first = value.astype(jnp.bfloat16).astype(jnp.float32)
    rest = value - first
    second = rest.astype(jnp.bfloat16).astype(jnp.float32)
    return [first, second, rest - second]


def aux_tile(total, peak):
    pad = jnp.zeros((AUX - 6, LANES), jnp.float32)
    return jnp.concatenate(three(total) + three(peak) + [pad], axis=0).astype(jnp.bfloat16)


def attend_kernel(blocks, shards, per, width, masked, where_ref, *refs):
    packs, slabs = refs[:blocks], refs[blocks : blocks + shards]
    outs = refs[blocks + shards : 2 * blocks + shards]
    keys = refs[2 * blocks + shards]
    rows = blocks * per
    tokens = slabs[0].shape[1]
    runs = tokens // RUN
    span = RUN * RUN
    his = packs[0].shape[1] - width
    hi_at = lax.broadcasted_iota(jnp.int32, (his, LANES), 0)
    lane_at = lax.broadcasted_iota(jnp.int32, (RUN, span), 1).astype(jnp.float32)
    tables = [
        packs[row // per][row % per, width:, :].astype(jnp.float32) for row in range(rows)
    ]
    valid = []
    for shard in range(shards):
        own = [
            jnp.sum(jnp.where(hi_at == where_ref[2 * shard], table, 0.0), axis=0, keepdims=True)
            for table in tables
        ]
        line = jnp.concatenate(own, axis=0)
        line = jnp.where(where_ref[2 * shard + 1] == 1, pltpu.roll(line, runs, 1), line)
        column = jnp.transpose(line)[:runs, :]
        base = (lax.broadcasted_iota(jnp.int32, column.shape, 0) % RUN * RUN).astype(jnp.float32)
        target = jnp.where(column > 0.0, base + column - 1.0, -1.0)
        valid.append(column)
        for at in range(runs // RUN):
            hits = [
                (lane_at == target[at * RUN : (at + 1) * RUN, row : row + 1])
                .astype(jnp.float32)
                .astype(jnp.bfloat16)
                for row in range(rows)
            ]
            picked = lax.dot_general(
                jnp.concatenate(hits, axis=0),
                slabs[shard][:, at * span : (at + 1) * span],
                (((1,), (1,)), ((), ())),
                preferred_element_type=jnp.float32,
            ).astype(jnp.bfloat16)
            start = shard * runs + at * RUN
            keys[:, start : start + RUN, :] = picked.reshape(rows, RUN, width)
    for row in range(rows):
        block, at = row // per, row % per
        mine = keys[row]
        scores = jnp.dot(mine, packs[block][at, :width, :], preferred_element_type=jnp.float32)
        if masked:
            known = jnp.concatenate([v[:, row : row + 1] for v in valid], axis=0) > 0.0
            known = jnp.broadcast_to(known, scores.shape)
            scores = jnp.where(known, scores, -1e30)
        top = jnp.max(scores, axis=0, keepdims=True)
        weights = jnp.exp2((scores - top) * SCALE)
        if masked:
            weights = jnp.where(known, weights, 0.0)
        weights = weights.astype(jnp.bfloat16)
        total = jnp.sum(weights.astype(jnp.float32), axis=0, keepdims=True)
        sums = lax.dot_general(
            weights, mine[:, :LATENT], (((0,), (0,)), ((), ())), preferred_element_type=jnp.float32
        )
        heads = sums.shape[0]
        outs[block][at * heads : (at + 1) * heads, :] = sums.astype(jnp.bfloat16)
        outs[block][per * heads :, at * LANES : (at + 1) * LANES] = aux_tile(total, top * SCALE)


def attend(packs, slabs, where, width, masked):
    blocks, shards = len(packs), len(slabs)
    per, _, heads = packs[0].shape
    slots = shards * (slabs[0].shape[1] // RUN)
    rows = blocks * per
    out = jax.ShapeDtypeStruct((per * heads + AUX, LATENT), jnp.bfloat16)
    return pl.pallas_call(
        functools.partial(attend_kernel, blocks, shards, per, width, masked),
        out_shape=[out] * blocks,
        in_specs=[pl.BlockSpec(memory_space=pltpu.SMEM)] + whole_vmem(blocks + shards),
        out_specs=whole_vmem(blocks),
        scratch_shapes=[pltpu.VMEM((rows, slots, width), jnp.bfloat16)],
        compiler_params=params(),
        cost_estimate=pl.CostEstimate(
            flops=2 * rows * slots * (heads * (width + LATENT) + RUN * RUN * width),
            bytes_accessed=rows * heads * (width + LATENT) * 2 + shards * slabs[0].size * 2,
            transcendentals=rows * slots * heads,
        ),
        name="attend",
    )(where, *packs, *slabs)


def combine_kernel(per, heads, last, *refs):
    parts, out = refs[:-1], refs[-1]
    for at in range(per):
        lanes = pl.ds(at * LANES, LANES)
        totals, peaks = [], []
        for part in parts:
            aux = part[per * heads :, lanes].astype(jnp.float32)
            totals.append(aux[0:1] + aux[1:2] + aux[2:3])
            peaks.append(aux[3:4] + aux[4:5] + aux[5:6])
        peak = functools.reduce(jnp.maximum, peaks)
        shares = [jnp.exp2(p - peak) for p in peaks]
        total = functools.reduce(jnp.add, [s * t for s, t in zip(shares, totals)])
        if last:
            shares = [s / total for s in shares]
        pad = -len(shares) % 8
        columns = jnp.transpose(
            jnp.concatenate(shares + [jnp.zeros((pad, LANES), jnp.float32)] * (pad > 0), axis=0)
        )
        mixed = None
        for i, part in enumerate(parts):
            term = part[at * heads : (at + 1) * heads, :].astype(jnp.float32) * columns[:, i : i + 1]
            mixed = term if mixed is None else mixed + term
        if last:
            out[at] = mixed.astype(jnp.bfloat16)
        else:
            out[at * heads : (at + 1) * heads, :] = mixed.astype(jnp.bfloat16)
            out[per * heads :, lanes] = aux_tile(total, peak)


def combine(parts, per, last):
    heads = (parts[0].shape[0] - AUX) // per
    shape = (per, heads, LATENT) if last else parts[0].shape
    return pl.pallas_call(
        functools.partial(combine_kernel, per, heads, last),
        out_shape=jax.ShapeDtypeStruct(shape, jnp.bfloat16),
        in_specs=whole_vmem(len(parts)),
        out_specs=pl.BlockSpec(memory_space=VMEM),
        compiler_params=params(),
        name="combine",
    )(*parts)


def index_block(iquery, gates, index_keys):
    count, heads, size = iquery.shape
    groups = count // 8
    query_blocks = iquery.reshape(groups, 8 * heads, size)
    gate_blocks = gates.astype(jnp.float32).reshape(groups, 8, heads)

    def one_block(pair):
        block, gate = pair
        logits = jnp.einsum("qd,td->qt", block, index_keys, preferred_element_type=jnp.float32)
        logits = logits.reshape(8, heads, logits.shape[1])
        return jnp.sum(gate[:, :, None] * jnp.maximum(logits, 0.0), axis=1)

    result = lax.map(one_block, (query_blocks, gate_blocks))
    return result.reshape(count, result.shape[2])


def solution(mesh):
    columns, planes = mesh.shape["ctx"], mesh.shape["row"]
    chips = columns // 2
    token_masks = [1] if planes > 1 else []
    row_masks = list(range(2, planes, 2))

    def swap(array, axis, mask):
        size = mesh.shape[axis]
        return lax.ppermute(array, axis, [(i, i ^ mask) for i in range(size)])

    def body(latent_cache, index_keys, query_latent, index_query, index_gates, selected):
        here, plane = lax.axis_index("ctx"), lax.axis_index("row")
        per, _, width = query_latent.shape
        tokens = latent_cache.shape[0]
        all_runs = tokens * columns * planes // RUN
        his = all_runs // LANES
        masked = all_runs != selected.shape[1]
        slab = jnp.swapaxes(latent_cache, 0, 1)
        query = jnp.swapaxes(query_latent, 1, 2)

        packed = with_table(query, selected, his)
        slabs, where = [], []
        for mask in [0] + token_masks:
            one = swap(slab, "row", mask) if mask else slab
            slabs += [one, swap(one, "ctx", 1)]
            for column in (here, here ^ 1):
                start = (column * planes + (plane ^ mask)) * (tokens // RUN)
                where += [start // LANES, start % LANES // (tokens // RUN)]
        where = jnp.stack(where).astype(jnp.int32)

        groups = {}
        for mask in row_masks + [0]:
            first = swap(packed, "row", mask) if mask else packed
            groups[mask] = [first] + [swap(first, "ctx", 2 * p) for p in range(1, chips)]

        iquery = lax.all_gather(index_query, "ctx", axis=0, tiled=True)
        gates = lax.all_gather(index_gates, "ctx", axis=0, tiled=True)
        index_scores = index_block(iquery, gates, index_keys)

        parts = []
        for mask in row_masks + [0]:
            packs, done = groups[mask], []
            step = min(4, chips)
            for at in range(0, chips, step):
                done += attend(packs[at : at + step], slabs, where, width, masked)
            mine = [done[0]] + [swap(done[p], "ctx", 2 * p) for p in range(1, chips)]
            if mask:
                parts.append(swap(combine(mine, per, False), "row", mask))
            else:
                parts += mine
        attended = combine(parts, per, True)
        return attended, index_scores

    return jax.shard_map(
        body,
        mesh=mesh,
        in_specs=(
            P(("ctx", "row"), None),
            P("ctx", None),
            P(("row", "ctx"), None, None),
            P(("row", "ctx"), None, None),
            P(("row", "ctx"), None),
            P(("row", "ctx"), None),
        ),
        out_specs=(P(("row", "ctx"), None, None), P("row", "ctx")),
        check_vma=False,
    )
```

```python
import functools

import jax
import jax.numpy as jnp
from jax import lax
from jax.experimental import pallas as pl
from jax.experimental.pallas import tpu as pltpu
from jax.sharding import PartitionSpec as P

LATENT = 512
SCORE_DIM = 192
SEL_MOST = 256
TOK_DEV = 4096
RUN = TOK_DEV // SEL_MOST
LANES = 128
AUX = 16
BATCH = 4
SCALE = SCORE_DIM ** (-0.5) * 1.4426950408889634
VMEM = pltpu.VMEM
TINY = pl.CostEstimate(flops=1000, bytes_accessed=1000, transcendentals=0)


def whole_vmem(count):
    return [pl.BlockSpec(memory_space=VMEM)] * count


def params(mib):
    return pltpu.CompilerParams(vmem_limit_bytes=mib * 1024 * 1024)


def near(arrays):
    return [pltpu.with_memory_space_constraint(a, VMEM) for a in arrays]


def table_kernel(query_ref, selected_ref, out_ref):
    rows, width, _ = query_ref.shape
    his = out_ref.shape[1] - width
    picks = selected_ref.shape[1]
    hi_at = lax.broadcasted_iota(jnp.int32, (his, picks), 0)
    lo_at = lax.broadcasted_iota(jnp.int32, (LANES, picks), 0)
    out_ref[:, :width, :] = query_ref[...]
    for row in range(rows):
        token = selected_ref[row : row + 1, :]
        offset = (token % RUN + 1).astype(jnp.float32)
        run = token // RUN
        high = (hi_at == run // LANES).astype(jnp.float32).astype(jnp.bfloat16)
        low = jnp.where(lo_at == run % LANES, offset, 0.0).astype(jnp.bfloat16)
        table = lax.dot_general(
            high, low, (((1,), (1,)), ((), ())), preferred_element_type=jnp.float32
        )
        out_ref[row, width:, :] = table.astype(jnp.bfloat16)


def with_table(query, selected, his):
    rows, width, heads = query.shape
    return pl.pallas_call(
        table_kernel,
        out_shape=jax.ShapeDtypeStruct((rows, width + his, heads), jnp.bfloat16),
        in_specs=whole_vmem(2),
        out_specs=pl.BlockSpec(memory_space=VMEM),
        compiler_params=params(8),
        cost_estimate=TINY,
        name="table",
    )(query, selected)


def three(value):
    first = value.astype(jnp.bfloat16).astype(jnp.float32)
    rest = value - first
    second = rest.astype(jnp.bfloat16).astype(jnp.float32)
    return [first, second, rest - second]


def aux_tile(total, peak):
    pad = jnp.zeros((AUX - 6, LANES), jnp.float32)
    return jnp.concatenate(three(total) + three(peak) + [pad], axis=0).astype(jnp.bfloat16)


def attend_kernel(blocks, shards, per, width, masked, where_ref, *refs):
    packs, slabs = refs[:blocks], refs[blocks : blocks + shards]
    outs = refs[blocks + shards : 2 * blocks + shards]
    keys = refs[2 * blocks + shards]
    rows = blocks * per
    span = RUN * RUN
    his = packs[0].shape[1] - width
    hi_at = lax.broadcasted_iota(jnp.int32, (his, LANES), 0)
    lane_at = lax.broadcasted_iota(jnp.int32, (RUN, span), 1).astype(jnp.float32)
    tables = [
        packs[row // per][row % per, width:, :].astype(jnp.float32) for row in range(rows)
    ]
    valid, begin = [], 0
    for shard in range(shards):
        runs = slabs[shard].shape[1] // RUN
        own = [
            jnp.sum(jnp.where(hi_at == where_ref[2 * shard], table, 0.0), axis=0, keepdims=True)
            for table in tables
        ]
        line = jnp.concatenate(own, axis=0)
        line = pltpu.roll(line, where_ref[2 * shard + 1], 1)
        column = jnp.transpose(line)[:runs, :]
        base = (lax.broadcasted_iota(jnp.int32, column.shape, 0) % RUN * RUN).astype(jnp.float32)
        target = jnp.where(column > 0.0, base + column - 1.0, -1.0)
        valid.append(column)
        for at in range(runs // RUN):
            hits = [
                (lane_at == target[at * RUN : (at + 1) * RUN, row : row + 1])
                .astype(jnp.float32)
                .astype(jnp.bfloat16)
                for row in range(rows)
            ]
            picked = lax.dot_general(
                jnp.concatenate(hits, axis=0),
                slabs[shard][:, at * span : (at + 1) * span],
                (((1,), (1,)), ((), ())),
                preferred_element_type=jnp.float32,
            ).astype(jnp.bfloat16)
            start = begin + at * RUN
            keys[:, start : start + RUN, :] = picked.reshape(rows, RUN, width)
        begin += runs
    for first in range(0, rows, BATCH):
        group = range(first, min(first + BATCH, rows))
        logits = [
            jnp.dot(
                keys[row],
                packs[row // per][row % per, :width, :],
                preferred_element_type=jnp.float32,
            )
            for row in group
        ]
        done = []
        for row, scores in zip(group, logits):
            if masked:
                known = jnp.concatenate([v[:, row : row + 1] for v in valid], axis=0) > 0.0
                known = jnp.broadcast_to(known, scores.shape)
                scores = jnp.where(known, scores, -1e30)
            top = jnp.max(scores, axis=0, keepdims=True)
            weights = jnp.exp2((scores - top) * SCALE)
            if masked:
                weights = jnp.where(known, weights, 0.0)
            weights = weights.astype(jnp.bfloat16)
            total = jnp.sum(weights.astype(jnp.float32), axis=0, keepdims=True)
            done.append((weights, total, top * SCALE))
        for row, (weights, total, peak) in zip(group, done):
            block, at = row // per, row % per
            sums = lax.dot_general(
                weights,
                keys[row, :, :LATENT],
                (((0,), (0,)), ((), ())),
                preferred_element_type=jnp.float32,
            )
            heads = sums.shape[0]
            outs[block][at * heads : (at + 1) * heads, :] = sums.astype(jnp.bfloat16)
            outs[block][per * heads :, at * LANES : (at + 1) * LANES] = aux_tile(total, peak)


def attend(packs, slabs, where, width, masked):
    blocks, shards = len(packs), len(slabs)
    per, _, heads = packs[0].shape
    slots = sum(slab.shape[1] for slab in slabs) // RUN
    rows = blocks * per
    out = VMEM((per * heads + AUX, LATENT), jnp.bfloat16)
    return pl.pallas_call(
        functools.partial(attend_kernel, blocks, shards, per, width, masked),
        out_shape=[out] * blocks,
        in_specs=[pl.BlockSpec(memory_space=pltpu.SMEM)] + whole_vmem(blocks + shards),
        out_specs=whole_vmem(blocks),
        scratch_shapes=[pltpu.VMEM((rows, slots, width), jnp.bfloat16)],
        compiler_params=params(14),
        cost_estimate=TINY,
        name="attend",
    )(where, *near(packs), *near(slabs))


def combine_kernel(per, heads, last, *refs):
    parts, out = refs[:-1], refs[-1]
    for at in range(per):
        lanes = pl.ds(at * LANES, LANES)
        totals, peaks = [], []
        for part in parts:
            aux = part[per * heads :, lanes].astype(jnp.float32)
            totals.append(aux[0:1] + aux[1:2] + aux[2:3])
            peaks.append(aux[3:4] + aux[4:5] + aux[5:6])
        peak = functools.reduce(jnp.maximum, peaks)
        shares = [jnp.exp2(p - peak) for p in peaks]
        total = functools.reduce(jnp.add, [s * t for s, t in zip(shares, totals)])
        if last:
            shares = [s / total for s in shares]
        pad = -len(shares) % 8
        columns = jnp.transpose(
            jnp.concatenate(shares + [jnp.zeros((pad, LANES), jnp.float32)] * (pad > 0), axis=0)
        )
        mixed = None
        for i, part in enumerate(parts):
            term = part[at * heads : (at + 1) * heads, :].astype(jnp.float32) * columns[:, i : i + 1]
            mixed = term if mixed is None else mixed + term
        if last:
            out[at] = mixed.astype(jnp.bfloat16)
        else:
            out[at * heads : (at + 1) * heads, :] = mixed.astype(jnp.bfloat16)
            out[per * heads :, lanes] = aux_tile(total, peak)


def combine(parts, per, last):
    heads = (parts[0].shape[0] - AUX) // per
    if last:
        out = jax.ShapeDtypeStruct((per, heads, LATENT), jnp.bfloat16)
    else:
        out = VMEM(parts[0].shape, jnp.bfloat16)
    return pl.pallas_call(
        functools.partial(combine_kernel, per, heads, last),
        out_shape=out,
        in_specs=whole_vmem(len(parts)),
        out_specs=pl.BlockSpec(memory_space=VMEM),
        compiler_params=params(8),
        cost_estimate=TINY,
        name="combine",
    )(*near(parts))


def index_kernel(heads, meta_ref, keys_ref, out_ref, gate_scr):
    rows = meta_ref.shape[0]
    tokens = keys_ref.shape[0]

    @pl.when(pl.program_id(0) == 0)
    def _():
        for first in range(0, rows, 8):
            lines = jnp.concatenate(
                [meta_ref[first + i, heads : heads + 8, :].astype(jnp.float32)[:1] for i in range(8)],
                axis=0,
            )
            turned = jnp.transpose(lines)
            for i in range(8):
                gate_scr[first + i] = jnp.broadcast_to(turned[:heads, i : i + 1], (heads, LANES))

    for first in range(0, rows, 8):
        queries = jnp.concatenate([meta_ref[first + i, :heads, :] for i in range(8)], axis=0)
        logits = lax.dot_general(
            queries, keys_ref[...], (((1,), (1,)), ((), ())), preferred_element_type=jnp.float32
        )
        lines = []
        for i in range(8):
            gate = jnp.concatenate([gate_scr[first + i]] * (tokens // LANES), axis=1)
            terms = jnp.maximum(logits[i * heads : (i + 1) * heads, :], 0.0) * gate
            lines.append(jnp.sum(terms, axis=0, keepdims=True))
        out_ref[first : first + 8, :] = jnp.concatenate(lines, axis=0)


def index_block(meta, index_keys, heads):
    rows, tall, size = meta.shape
    tokens = index_keys.shape[0]
    block = 512
    return pl.pallas_call(
        functools.partial(index_kernel, heads),
        grid=(tokens // block,),
        out_shape=jax.ShapeDtypeStruct((rows, tokens), jnp.float32),
        in_specs=[
            pl.BlockSpec((rows, tall, size), lambda i: (0, 0, 0)),
            pl.BlockSpec((block, size), lambda i: (i, 0)),
        ],
        out_specs=pl.BlockSpec((rows, block), lambda i: (0, i)),
        scratch_shapes=[VMEM((rows, heads, LANES), jnp.float32)],
        compiler_params=params(14),
        cost_estimate=TINY,
        name="index",
    )(meta, index_keys)


def solution(mesh):
    columns, planes = mesh.shape["ctx"], mesh.shape["row"]
    token_columns = [0, 2] if columns > 2 else [0]
    token_planes = [0, 1] if planes > 1 else [0]
    row_columns = list(range(0, columns, 4))
    row_planes = list(range(0, planes, 2))

    def swap(array, axis, mask):
        size = mesh.shape[axis]
        return lax.ppermute(array, axis, [(i, i ^ mask) for i in range(size)])

    def body(latent_cache, index_keys, query_latent, index_query, index_gates, selected):
        here, plane = lax.axis_index("ctx"), lax.axis_index("row")
        per, _, width = query_latent.shape
        heads = index_query.shape[1]
        tokens = latent_cache.shape[0]
        runs = tokens // RUN
        all_runs = runs * columns * planes
        masked = all_runs != selected.shape[1]
        slab = jnp.swapaxes(latent_cache, 0, 1)
        query = jnp.swapaxes(query_latent, 1, 2)

        def after(array, *others):
            return lax.optimization_barrier((array, *others))[0]

        gate_rows = jnp.pad(
            index_gates[:, None, :], ((0, 0), (0, AUX - 1), (0, LANES - index_gates.shape[1]))
        )
        meta = jnp.concatenate([index_query, gate_rows], axis=1)
        bit = 1
        while bit < columns:
            other = swap(meta, "ctx", bit)
            low, high = jnp.concatenate([meta, other]), jnp.concatenate([other, meta])
            meta = jnp.where(here & bit == 0, low, high)
            bit *= 2

        packed = with_table(query, selected, all_runs // LANES)
        starts = {across: swap(packed, "row", across) if across else packed for across in row_planes}
        groups = {
            across: {mask: swap(start, "ctx", mask) if mask else start for mask in row_columns}
            for across, start in starts.items()
        }
        near_queries = list(groups[0].values()) + list(starts.values())
        far_queries = [pack for group in groups.values() for pack in group.values()]
        index_scores = index_block(after(meta, *near_queries), index_keys, heads)

        half = tokens // 2
        pieces, sent, shown = [(0, 0, slab)], [], []
        for across in token_planes[1:]:
            for offset in (0, half):
                piece = slab[:, offset : offset + half]
                sent.append(swap(after(piece, *sent[-1:]), "row", across))
                pieces.append((across, offset, sent[-1]))
        slabs, where = [], []
        for across, offset, piece in pieces:
            for mask in token_columns:
                one = piece
                if mask:
                    late = list(starts.values()) if offset else []
                    one = swap(after(piece, *late, *shown[-1:]), "ctx", mask)
                    shown.append(one)
                for core in (0, 1):
                    if core and mask and offset:
                        one = after(one, index_scores, *far_queries)
                    slabs.append(swap(one, "ctx", 1) if core else one)
                    start = (here ^ mask ^ core) * planes + (plane ^ across)
                    start = (start * tokens + offset) // RUN
                    where += [start // LANES, (-start) % LANES]
        where = jnp.stack(where).astype(jnp.int32)

        parts, last = [], after(where, index_scores)
        for across in row_planes[1:] + row_planes[:1]:
            mine = []
            for mask in reversed(row_columns):
                (done,) = attend([groups[across][mask]], slabs, last, width, masked)
                last = after(where, done)
                mine.append(swap(done, "ctx", mask) if mask else done)
            if across:
                parts.append(swap(combine(mine, per, False), "row", across))
            else:
                parts += mine
        attended = combine(parts, per, True)
        return attended, index_scores

    return jax.shard_map(
        body,
        mesh=mesh,
        in_specs=(
            P(("ctx", "row"), None),
            P("ctx", None),
            P(("row", "ctx"), None, None),
            P(("row", "ctx"), None, None),
            P(("row", "ctx"), None),
            P(("row", "ctx"), None),
        ),
        out_specs=(P(("row", "ctx"), None, None), P("row", "ctx")),
        check_vma=False,
    )
```

```python
import functools

import jax
import jax.numpy as jnp
from jax import lax
from jax.experimental import pallas as pl
from jax.experimental.pallas import tpu as pltpu
from jax.sharding import PartitionSpec as P

LATENT = 512
SCORE_DIM = 192
SEL_MOST = 256
TOK_DEV = 4096
RUN = TOK_DEV // SEL_MOST
LANES = 128
AUX = 16
BATCH = 4
SCALE = SCORE_DIM ** (-0.5) * 1.4426950408889634
VMEM = pltpu.VMEM
LONG = pl.CostEstimate(flops=1000, bytes_accessed=60000000, transcendentals=0)
TINY = pl.CostEstimate(flops=1000, bytes_accessed=1000, transcendentals=0)


def whole_vmem(count):
    return [pl.BlockSpec(memory_space=VMEM)] * count


def params(mib):
    return pltpu.CompilerParams(vmem_limit_bytes=mib * 1024 * 1024)


def near(arrays):
    return [pltpu.with_memory_space_constraint(a, VMEM) for a in arrays]


def table_kernel(query_ref, selected_ref, out_ref):
    rows, width, _ = query_ref.shape
    his = out_ref.shape[1] - width
    picks = selected_ref.shape[1]
    hi_at = lax.broadcasted_iota(jnp.int32, (his, picks), 0)
    lo_at = lax.broadcasted_iota(jnp.int32, (LANES, picks), 0)
    out_ref[:, :width, :] = query_ref[...]
    for row in range(rows):
        token = selected_ref[row : row + 1, :]
        offset = (token % RUN + 1).astype(jnp.float32)
        run = token // RUN
        high = (hi_at == run // LANES).astype(jnp.float32).astype(jnp.bfloat16)
        low = jnp.where(lo_at == run % LANES, offset, 0.0).astype(jnp.bfloat16)
        table = lax.dot_general(
            high, low, (((1,), (1,)), ((), ())), preferred_element_type=jnp.float32
        )
        out_ref[row, width:, :] = table.astype(jnp.bfloat16)


def with_table(query, selected, his):
    rows, width, heads = query.shape
    return pl.pallas_call(
        table_kernel,
        out_shape=jax.ShapeDtypeStruct((rows, width + his, heads), jnp.bfloat16),
        in_specs=whole_vmem(2),
        out_specs=pl.BlockSpec(memory_space=VMEM),
        compiler_params=params(8),
        cost_estimate=TINY,
        name="table",
    )(query, selected)


def three(value):
    first = value.astype(jnp.bfloat16).astype(jnp.float32)
    rest = value - first
    second = rest.astype(jnp.bfloat16).astype(jnp.float32)
    return [first, second, rest - second]


def aux_tile(total, peak):
    pad = jnp.zeros((AUX - 6, LANES), jnp.float32)
    return jnp.concatenate(three(total) + three(peak) + [pad], axis=0).astype(jnp.bfloat16)


def attend_kernel(blocks, shards, per, width, masked, parts, where_ref, *refs):
    packs, slabs = refs[:blocks], refs[blocks : blocks + shards]
    outs, keys = refs[blocks + shards : -1], refs[-1]
    some = per // parts
    rows = blocks * per
    span = RUN * RUN
    his = packs[0].shape[1] - width
    hi_at = lax.broadcasted_iota(jnp.int32, (his, LANES), 0)
    lane_at = lax.broadcasted_iota(jnp.int32, (RUN, span), 1).astype(jnp.float32)
    tables = [
        packs[row // per][row % per, width:, :].astype(jnp.float32) for row in range(rows)
    ]
    valid, begin = [], 0
    for shard in range(shards):
        runs = slabs[shard].shape[1] // RUN
        own = [
            jnp.sum(jnp.where(hi_at == where_ref[2 * shard], table, 0.0), axis=0, keepdims=True)
            for table in tables
        ]
        line = jnp.concatenate(own, axis=0)
        line = pltpu.roll(line, where_ref[2 * shard + 1], 1)
        column = jnp.transpose(line)[:runs, :]
        base = (lax.broadcasted_iota(jnp.int32, column.shape, 0) % RUN * RUN).astype(jnp.float32)
        target = jnp.where(column > 0.0, base + column - 1.0, -1.0)
        valid.append(column)
        for at in range(runs // RUN):
            hits = [
                (lane_at == target[at * RUN : (at + 1) * RUN, row : row + 1])
                .astype(jnp.float32)
                .astype(jnp.bfloat16)
                for row in range(rows)
            ]
            picked = lax.dot_general(
                jnp.concatenate(hits, axis=0),
                slabs[shard][:, at * span : (at + 1) * span],
                (((1,), (1,)), ((), ())),
                preferred_element_type=jnp.float32,
            ).astype(jnp.bfloat16)
            start = begin + at * RUN
            keys[:, start : start + RUN, :] = picked.reshape(rows, RUN, width)
        begin += runs
    for first in range(0, rows, BATCH):
        group = range(first, min(first + BATCH, rows))
        logits = [
            jnp.dot(
                keys[row],
                packs[row // per][row % per, :width, :],
                preferred_element_type=jnp.float32,
            )
            for row in group
        ]
        done = []
        for row, scores in zip(group, logits):
            if masked:
                known = jnp.concatenate([v[:, row : row + 1] for v in valid], axis=0) > 0.0
                known = jnp.broadcast_to(known, scores.shape)
                scores = jnp.where(known, scores, -1e30)
            top = jnp.max(scores, axis=0, keepdims=True)
            weights = jnp.exp2((scores - top) * SCALE)
            if masked:
                weights = jnp.where(known, weights, 0.0)
            weights = weights.astype(jnp.bfloat16)
            total = jnp.sum(weights.astype(jnp.float32), axis=0, keepdims=True)
            done.append((weights, total, top * SCALE))
        for row, (weights, total, peak) in zip(group, done):
            block, at = row // per, row % per
            sums = lax.dot_general(
                weights,
                keys[row, :, :LATENT],
                (((0,), (0,)), ((), ())),
                preferred_element_type=jnp.float32,
            )
            heads = sums.shape[0]
            out, at = outs[block * parts + at // some], at % some
            out[at * heads : (at + 1) * heads, :] = sums.astype(jnp.bfloat16)
            out[some * heads :, at * LANES : (at + 1) * LANES] = aux_tile(total, peak)


def attend(packs, slabs, where, width, masked, parts):
    blocks, shards = len(packs), len(slabs)
    per, _, heads = packs[0].shape
    slots = sum(slab.shape[1] for slab in slabs) // RUN
    rows = blocks * per
    out = VMEM((per // parts * heads + AUX, LATENT), jnp.bfloat16)
    return pl.pallas_call(
        functools.partial(attend_kernel, blocks, shards, per, width, masked, parts),
        out_shape=[out] * (blocks * parts),
        in_specs=[pl.BlockSpec(memory_space=pltpu.SMEM)] + whole_vmem(blocks + shards),
        out_specs=whole_vmem(blocks * parts),
        scratch_shapes=[pltpu.VMEM((rows, slots, width), jnp.bfloat16)],
        compiler_params=params(14),
        cost_estimate=TINY,
        name="attend",
    )(where, *near(packs), *near(slabs))


def combine_kernel(begins, rows, heads, last, *refs):
    parts, out = refs[: len(begins)], refs[-1]
    for row in rows:
        blocks, totals, peaks = [], [], []
        for ref, begin in zip(parts, begins):
            some, at = (ref.shape[0] - AUX) // heads, row - begin
            aux = ref[some * heads :, at * LANES : (at + 1) * LANES].astype(jnp.float32)
            totals.append(aux[0:1] + aux[1:2] + aux[2:3])
            peaks.append(aux[3:4] + aux[4:5] + aux[5:6])
            blocks.append(ref[at * heads : (at + 1) * heads, :].astype(jnp.float32))
        peak = functools.reduce(jnp.maximum, peaks)
        shares = [jnp.exp2(p - peak) for p in peaks]
        total = functools.reduce(jnp.add, [s * t for s, t in zip(shares, totals)])
        if last:
            shares = [s / total for s in shares]
        pad = -len(shares) % 8
        columns = jnp.transpose(
            jnp.concatenate(shares + [jnp.zeros((pad, LANES), jnp.float32)] * (pad > 0), axis=0)
        )
        terms = [block * columns[:, i : i + 1] for i, block in enumerate(blocks)]
        mixed = functools.reduce(jnp.add, terms).astype(jnp.bfloat16)
        at = row - rows[0]
        if last:
            out[at] = mixed
        else:
            out[at * heads : (at + 1) * heads, :] = mixed
            out[len(rows) * heads :, at * LANES : (at + 1) * LANES] = aux_tile(total, peak)


def combine(parts, begins, rows, heads):
    return pl.pallas_call(
        functools.partial(combine_kernel, begins, rows, heads, False),
        out_shape=VMEM((len(rows) * heads + AUX, LATENT), jnp.bfloat16),
        in_specs=whole_vmem(len(parts)),
        out_specs=pl.BlockSpec(memory_space=VMEM),
        compiler_params=params(8),
        cost_estimate=TINY,
        name="combine",
    )(*near(parts))


def finish(parts, begins, rows, per, heads, done, cost):
    count, at = len(rows), rows[0] // len(rows)
    more = [] if done is None else [done]
    return pl.pallas_call(
        functools.partial(combine_kernel, begins, rows, heads, True),
        grid=(1,),
        out_shape=jax.ShapeDtypeStruct((per, heads, LATENT), jnp.bfloat16),
        in_specs=whole_vmem(len(parts)) + [pl.BlockSpec(memory_space=pl.ANY)] * len(more),
        out_specs=pl.BlockSpec((count, heads, LATENT), lambda i: (at, 0, 0)),
        input_output_aliases={len(parts): 0} if more else {},
        compiler_params=params(8),
        cost_estimate=cost,
        name="finish",
    )(*near(parts), *more)


def index_kernel(heads, meta_ref, keys_ref, out_ref, gate_scr):
    rows = meta_ref.shape[0]
    tokens = keys_ref.shape[0]

    @pl.when(pl.program_id(0) == 0)
    def _():
        for first in range(0, rows, 8):
            lines = jnp.concatenate(
                [meta_ref[first + i, heads : heads + 8, :].astype(jnp.float32)[:1] for i in range(8)],
                axis=0,
            )
            turned = jnp.transpose(lines)
            for i in range(8):
                gate_scr[first + i] = jnp.broadcast_to(turned[:heads, i : i + 1], (heads, LANES))

    for first in range(0, rows, 8):
        queries = jnp.concatenate([meta_ref[first + i, :heads, :] for i in range(8)], axis=0)
        logits = lax.dot_general(
            queries, keys_ref[...], (((1,), (1,)), ((), ())), preferred_element_type=jnp.float32
        )
        lines = []
        for i in range(8):
            gate = jnp.concatenate([gate_scr[first + i]] * (tokens // LANES), axis=1)
            terms = jnp.maximum(logits[i * heads : (i + 1) * heads, :], 0.0) * gate
            lines.append(jnp.sum(terms, axis=0, keepdims=True))
        out_ref[first : first + 8, :] = jnp.concatenate(lines, axis=0)


def index_block(meta, index_keys, heads):
    rows, tall, size = meta.shape
    tokens = index_keys.shape[0]
    block = 512
    return pl.pallas_call(
        functools.partial(index_kernel, heads),
        grid=(tokens // block,),
        out_shape=jax.ShapeDtypeStruct((rows, tokens), jnp.float32),
        in_specs=[
            pl.BlockSpec((rows, tall, size), lambda i: (0, 0, 0)),
            pl.BlockSpec((block, size), lambda i: (i, 0)),
        ],
        out_specs=pl.BlockSpec((rows, block), lambda i: (0, i)),
        scratch_shapes=[VMEM((rows, heads, LANES), jnp.float32)],
        compiler_params=params(14),
        cost_estimate=TINY,
        name="index",
    )(meta, index_keys)


def solution(mesh):
    columns, planes = mesh.shape["ctx"], mesh.shape["row"]
    token_columns = [0, 2] if columns > 2 else [0]
    token_planes = [0, 1] if planes > 1 else [0]
    row_columns = list(range(0, columns, 4))
    row_planes = list(range(0, planes, 2))

    def swap(array, axis, mask):
        size = mesh.shape[axis]
        return lax.ppermute(array, axis, [(i, i ^ mask) for i in range(size)])

    def body(latent_cache, index_keys, query_latent, index_query, index_gates, selected):
        here, plane = lax.axis_index("ctx"), lax.axis_index("row")
        per, _, width = query_latent.shape
        heads = query_latent.shape[1]
        tokens = latent_cache.shape[0]
        runs = tokens // RUN
        all_runs = runs * columns * planes
        masked = all_runs != selected.shape[1]
        slab = jnp.swapaxes(latent_cache, 0, 1)
        query = jnp.swapaxes(query_latent, 1, 2)

        def after(array, *others):
            return lax.optimization_barrier((array, *others))[0]

        gate_rows = jnp.pad(
            index_gates[:, None, :], ((0, 0), (0, AUX - 1), (0, LANES - index_gates.shape[1]))
        )
        meta = jnp.concatenate([index_query, gate_rows], axis=1)
        bit = 1
        while bit < columns:
            other = swap(meta, "ctx", bit)
            low, high = jnp.concatenate([meta, other]), jnp.concatenate([other, meta])
            meta = jnp.where(here & bit == 0, low, high)
            bit *= 2

        packed = with_table(query, selected, all_runs // LANES)
        starts = {across: swap(packed, "row", across) if across else packed for across in row_planes}
        groups = {
            across: {mask: swap(start, "ctx", mask) if mask else start for mask in row_columns}
            for across, start in starts.items()
        }
        near_queries = list(groups[0].values()) + list(starts.values())
        far_queries = [pack for group in groups.values() for pack in group.values()]
        index_scores = index_block(after(meta, *near_queries), index_keys, index_query.shape[1])

        half = tokens // 2
        pieces, sent, shown = [(0, 0, slab)], [], []
        for across in token_planes[1:]:
            for offset in (0, half):
                piece = slab[:, offset : offset + half]
                sent.append(swap(after(piece, *sent[-1:]), "row", across))
                pieces.append((across, offset, sent[-1]))
        slabs, where = [], []
        for across, offset, piece in pieces:
            for mask in token_columns:
                one = piece
                if mask:
                    late = list(starts.values()) if offset else []
                    one = swap(after(piece, *late, *shown[-1:]), "ctx", mask)
                    shown.append(one)
                for core in (0, 1):
                    if core and mask and offset:
                        one = after(one, index_scores, *far_queries)
                    slabs.append(swap(one, "ctx", 1) if core else one)
                    start = (here ^ mask ^ core) * planes + (plane ^ across)
                    start = (start * tokens + offset) // RUN
                    where += [start // LANES, (-start) % LANES]
        where = jnp.stack(where).astype(jnp.int32)

        parts, last = [], after(where, index_scores)
        split = 2
        some = per // split
        for across in row_planes[1:] + row_planes[:1]:
            mine = []
            for mask in reversed(row_columns):
                done = attend(
                    [groups[across][mask]], slabs, last, width, masked, split if across else 1
                )
                last = after(where, *done)
                first = [] if across else [back[0] for back in parts]
                mine.append([swap(after(a, *first), "ctx", mask) if mask else a for a in done])
            if across:
                back = []
                for i in range(split):
                    rows = range(i * some, (i + 1) * some)
                    mixed = combine([part[i] for part in mine], [rows[0]] * len(mine), rows, heads)
                    back.append(swap(after(mixed, *back), "row", across))
                    last = after(where, *done, mixed) if i == 0 else last
                parts.append(back)
            else:
                own = [part[0] for part in mine]
        attended = None
        for i in range(split):
            rows = range(i * some, (i + 1) * some)
            far = [back[i] for back in parts]
            begins = [rows[0]] * len(far) + [0] * len(own)
            cost = TINY if i == split - 1 else LONG
            attended = finish(far + own, begins, rows, per, heads, attended, cost)
        return attended, index_scores

    return jax.shard_map(
        body,
        mesh=mesh,
        in_specs=(
            P(("ctx", "row"), None),
            P("ctx", None),
            P(("row", "ctx"), None, None),
            P(("row", "ctx"), None, None),
            P(("row", "ctx"), None),
            P(("row", "ctx"), None),
        ),
        out_specs=(P(("row", "ctx"), None, None), P("row", "ctx")),
        check_vma=False,
    )
```

```python
import functools

import jax
import jax.numpy as jnp
from jax import lax
from jax.experimental import pallas as pl
from jax.experimental.pallas import tpu as pltpu
from jax.sharding import PartitionSpec as P

LATENT = 512
SCORE_DIM = 192
SEL_MOST = 256
TOK_DEV = 4096
RUN = TOK_DEV // SEL_MOST
LANES = 128
AUX = 16
BATCH = 4
SCALE = SCORE_DIM ** (-0.5) * 1.4426950408889634
VMEM = pltpu.VMEM
LONG = pl.CostEstimate(flops=1000, bytes_accessed=60000000, transcendentals=0)
TINY = pl.CostEstimate(flops=1000, bytes_accessed=1000, transcendentals=0)


def whole_vmem(count):
    return [pl.BlockSpec(memory_space=VMEM)] * count


def params(mib):
    return pltpu.CompilerParams(vmem_limit_bytes=mib * 1024 * 1024)


def near(arrays):
    return [pltpu.with_memory_space_constraint(a, VMEM) for a in arrays]


def table_kernel(query_ref, selected_ref, out_ref):
    rows, width, _ = query_ref.shape
    his = out_ref.shape[1] - width
    picks = selected_ref.shape[1]
    hi_at = lax.broadcasted_iota(jnp.int32, (his, picks), 0)
    lo_at = lax.broadcasted_iota(jnp.int32, (LANES, picks), 0)
    out_ref[:, :width, :] = query_ref[...]
    for row in range(rows):
        token = selected_ref[row : row + 1, :]
        offset = (token % RUN + 1).astype(jnp.float32)
        run = token // RUN
        high = (hi_at == run // LANES).astype(jnp.float32).astype(jnp.bfloat16)
        low = jnp.where(lo_at == run % LANES, offset, 0.0).astype(jnp.bfloat16)
        table = lax.dot_general(
            high, low, (((1,), (1,)), ((), ())), preferred_element_type=jnp.float32
        )
        out_ref[row, width:, :] = table.astype(jnp.bfloat16)


def with_table(query, selected, his):
    rows, width, heads = query.shape
    return pl.pallas_call(
        table_kernel,
        out_shape=jax.ShapeDtypeStruct((rows, width + his, heads), jnp.bfloat16),
        in_specs=whole_vmem(2),
        out_specs=pl.BlockSpec(memory_space=VMEM),
        compiler_params=params(8),
        cost_estimate=TINY,
        name="table",
    )(query, selected)


def three(value):
    first = value.astype(jnp.bfloat16).astype(jnp.float32)
    rest = value - first
    second = rest.astype(jnp.bfloat16).astype(jnp.float32)
    return [first, second, rest - second]


def aux_tile(total, peak):
    pad = jnp.zeros((AUX - 6, LANES), jnp.float32)
    return jnp.concatenate(three(total) + three(peak) + [pad], axis=0).astype(jnp.bfloat16)


def attend_kernel(places, blocks, per, width, sizes, masked, parts, *refs):
    shards = len(places)
    packs, slabs = refs[:blocks], refs[blocks : blocks + shards]
    outs, keys, table = refs[blocks + shards : -2], refs[-2], refs[-1]
    some = per // parts
    rows = blocks * per
    span = RUN * RUN
    here, plane = lax.axis_index("ctx"), lax.axis_index("row")
    planes, tokens = sizes
    for i, pack in enumerate(packs):
        table[i * per : (i + 1) * per] = pack[:, width:, :].astype(jnp.float32)
    spare = [jnp.zeros((-rows % 8, LANES), jnp.float32)] * (rows % 8 > 0)
    lane = lax.broadcasted_iota(jnp.int32, (rows + -rows % 8, LANES), 1)
    base = (lane % RUN * RUN - 1).astype(jnp.float32)
    spread = lax.broadcasted_iota(jnp.int32, (RUN, span), 1).astype(jnp.float32)
    targets, begin = [], 0
    for slab, (core, across, mask, offset) in zip(slabs, places):
        start = ((here ^ mask ^ core) * planes + (plane ^ across)) * (tokens // RUN) + offset // RUN
        row, shift = start // LANES, (LANES - start % LANES + begin) % LANES
        line = [table[i, pl.ds(row, 1), :] for i in range(rows)]
        line = pltpu.roll(jnp.concatenate(line + spare, axis=0), shift, 1)
        tile = line if begin % LANES == 0 else jnp.where(lane >= begin % LANES, line, tile)
        begin += slab.shape[1] // RUN
        if begin % LANES == 0:
            targets.append(jnp.transpose(jnp.where(tile > 0.0, base + tile, -1.0)))
    slot = 0
    for slab in slabs:
        for at in range(0, slab.shape[1], span):
            target = targets[slot // LANES][slot % LANES : slot % LANES + RUN, :]
            hits = [
                (spread == target[:, i : i + 1]).astype(jnp.float32).astype(jnp.bfloat16)
                for i in range(rows)
            ]
            picked = lax.dot_general(
                jnp.concatenate(hits, axis=0),
                slab[:, at : at + span],
                (((1,), (1,)), ((), ())),
                preferred_element_type=jnp.float32,
            ).astype(jnp.bfloat16)
            keys[:, slot : slot + RUN, :] = picked.reshape(rows, RUN, width)
            slot += RUN
    for first in range(0, rows, BATCH):
        group = range(first, min(first + BATCH, rows))
        logits = [
            jnp.dot(
                keys[row],
                packs[row // per][row % per, :width, :],
                preferred_element_type=jnp.float32,
            )
            for row in group
        ]
        done = []
        for row, scores in zip(group, logits):
            if masked:
                known = jnp.concatenate([t[:, row : row + 1] for t in targets], axis=0) >= 0.0
                known = jnp.broadcast_to(known, scores.shape)
                scores = jnp.where(known, scores, -1e30)
            top = jnp.max(scores, axis=0, keepdims=True)
            weights = jnp.exp2((scores - top) * SCALE)
            if masked:
                weights = jnp.where(known, weights, 0.0)
            weights = weights.astype(jnp.bfloat16)
            total = jnp.sum(weights.astype(jnp.float32), axis=0, keepdims=True)
            done.append((weights, total, top * SCALE))
        for row, (weights, total, peak) in zip(group, done):
            block, at = row // per, row % per
            sums = lax.dot_general(
                weights,
                keys[row, :, :LATENT],
                (((0,), (0,)), ((), ())),
                preferred_element_type=jnp.float32,
            )
            heads = sums.shape[0]
            out, at = outs[block * parts + at // some], at % some
            out[at * heads : (at + 1) * heads, :] = sums.astype(jnp.bfloat16)
            out[some * heads :, at * LANES : (at + 1) * LANES] = aux_tile(total, peak)


def attend(packs, slabs, places, width, sizes, masked, parts):
    blocks = len(packs)
    per, tall, heads = packs[0].shape
    slots = sum(slab.shape[1] for slab in slabs) // RUN
    out = VMEM((per // parts * heads + AUX, LATENT), jnp.bfloat16)
    return pl.pallas_call(
        functools.partial(attend_kernel, places, blocks, per, width, sizes, masked, parts),
        out_shape=[out] * (blocks * parts),
        in_specs=whole_vmem(blocks + len(slabs)),
        out_specs=whole_vmem(blocks * parts),
        scratch_shapes=[
            VMEM((blocks * per, slots, width), jnp.bfloat16),
            VMEM((blocks * per, tall - width, LANES), jnp.float32),
        ],
        compiler_params=params(14),
        cost_estimate=TINY,
        name="attend",
    )(*near(packs), *near(slabs))


def combine_kernel(begins, rows, heads, last, *refs):
    parts, out = refs[: len(begins)], refs[-1]
    for row in rows:
        blocks, totals, peaks = [], [], []
        for ref, begin in zip(parts, begins):
            some, at = (ref.shape[0] - AUX) // heads, row - begin
            aux = ref[some * heads :, at * LANES : (at + 1) * LANES].astype(jnp.float32)
            totals.append(aux[0:1] + aux[1:2] + aux[2:3])
            peaks.append(aux[3:4] + aux[4:5] + aux[5:6])
            blocks.append(ref[at * heads : (at + 1) * heads, :].astype(jnp.float32))
        peak = functools.reduce(jnp.maximum, peaks)
        shares = [jnp.exp2(p - peak) for p in peaks]
        total = functools.reduce(jnp.add, [s * t for s, t in zip(shares, totals)])
        if last:
            shares = [s / total for s in shares]
        pad = -len(shares) % 8
        columns = jnp.transpose(
            jnp.concatenate(shares + [jnp.zeros((pad, LANES), jnp.float32)] * (pad > 0), axis=0)
        )
        terms = [block * columns[:, i : i + 1] for i, block in enumerate(blocks)]
        mixed = functools.reduce(jnp.add, terms).astype(jnp.bfloat16)
        at = row - rows[0]
        if last:
            out[at] = mixed
        else:
            out[at * heads : (at + 1) * heads, :] = mixed
            out[len(rows) * heads :, at * LANES : (at + 1) * LANES] = aux_tile(total, peak)


def combine(parts, begins, rows, heads):
    return pl.pallas_call(
        functools.partial(combine_kernel, begins, rows, heads, False),
        out_shape=VMEM((len(rows) * heads + AUX, LATENT), jnp.bfloat16),
        in_specs=whole_vmem(len(parts)),
        out_specs=pl.BlockSpec(memory_space=VMEM),
        compiler_params=params(8),
        cost_estimate=TINY,
        name="combine",
    )(*near(parts))


def finish(parts, begins, rows, per, heads, done, cost):
    count, at = len(rows), rows[0] // len(rows)
    more = [] if done is None else [done]
    return pl.pallas_call(
        functools.partial(combine_kernel, begins, rows, heads, True),
        grid=(1,),
        out_shape=jax.ShapeDtypeStruct((per, heads, LATENT), jnp.bfloat16),
        in_specs=whole_vmem(len(parts)) + [pl.BlockSpec(memory_space=pl.ANY)] * len(more),
        out_specs=pl.BlockSpec((count, heads, LATENT), lambda i: (at, 0, 0)),
        input_output_aliases={len(parts): 0} if more else {},
        compiler_params=params(8),
        cost_estimate=cost,
        name="finish",
    )(*near(parts), *more)


def index_kernel(heads, per, meta_ref, keys_ref, out_ref, gate_scr):
    rows = meta_ref.shape[0]
    tokens = keys_ref.shape[0]

    @pl.when(pl.program_id(0) == 0)
    def _():
        for first in range(0, rows, 8):
            lines = jnp.concatenate(
                [meta_ref[first + i, heads : heads + 8, :].astype(jnp.float32)[:1] for i in range(8)],
                axis=0,
            )
            turned = jnp.transpose(lines)
            for i in range(8):
                gate_scr[first + i] = jnp.broadcast_to(turned[:heads, i : i + 1], (heads, LANES))

    for first in range(0, rows, 2 * per):
        queries = jnp.concatenate([meta_ref[first + i, :heads, :] for i in range(2 * per)], axis=0)
        logits = lax.dot_general(
            queries, keys_ref[...], (((1,), (1,)), ((), ())), preferred_element_type=jnp.float32
        )
        lines = []
        for i in range(2 * per):
            gate = jnp.concatenate([gate_scr[first + i]] * (tokens // LANES), axis=1)
            terms = jnp.maximum(logits[i * heads : (i + 1) * heads, :], 0.0) * gate
            lines.append(jnp.sum(terms, axis=0, keepdims=True))
        here = lax.axis_index("ctx")
        ours, mates = lines[:per], lines[per:]
        group = jnp.where(
            here % 2 == 0, jnp.concatenate(ours + mates, axis=0), jnp.concatenate(mates + ours, axis=0)
        )
        place = (here // 2) ^ (first // (2 * per))
        out_ref[pl.ds(pl.multiple_of(place * 2 * per, 2 * per), 2 * per), :] = group


def index_block(meta, index_keys, heads, per):
    rows, tall, size = meta.shape
    tokens = index_keys.shape[0]
    block = 512
    return pl.pallas_call(
        functools.partial(index_kernel, heads, per),
        grid=(tokens // block,),
        out_shape=jax.ShapeDtypeStruct((rows, tokens), jnp.float32),
        in_specs=[
            pl.BlockSpec((rows, tall, size), lambda i: (0, 0, 0)),
            pl.BlockSpec((block, size), lambda i: (i, 0)),
        ],
        out_specs=pl.BlockSpec((rows, block), lambda i: (0, i)),
        scratch_shapes=[VMEM((rows, heads, LANES), jnp.float32)],
        compiler_params=params(14),
        cost_estimate=TINY,
        name="index",
    )(meta, index_keys)


def solution(mesh):
    columns, planes = mesh.shape["ctx"], mesh.shape["row"]
    token_columns = [0, 2] if columns > 2 else [0]
    token_planes = [0, 1] if planes > 1 else [0]
    row_columns = list(range(0, columns, 4))
    row_planes = list(range(0, planes, 2))

    def swap(array, axis, mask):
        size = mesh.shape[axis]
        return lax.ppermute(array, axis, [(i, i ^ mask) for i in range(size)])

    def body(latent_cache, index_keys, query_latent, index_query, index_gates, selected):
        per, _, width = query_latent.shape
        heads = query_latent.shape[1]
        tokens = latent_cache.shape[0]
        runs = tokens // RUN
        all_runs = runs * columns * planes
        masked = all_runs != selected.shape[1]
        slab = jnp.swapaxes(latent_cache, 0, 1)
        query = jnp.swapaxes(query_latent, 1, 2)

        def after(array, *others):
            return lax.optimization_barrier((array, *others))[0]

        gate_rows = jnp.pad(
            index_gates[:, None, :], ((0, 0), (0, AUX - 1), (0, LANES - index_gates.shape[1]))
        )
        meta = jnp.concatenate([index_query, gate_rows], axis=1)
        bit = 1
        while bit < columns:
            other = swap(meta, "ctx", bit)
            meta = jnp.concatenate([meta, other])
            bit *= 2

        packed = with_table(query, selected, all_runs // LANES)
        starts = {across: swap(packed, "row", across) if across else packed for across in row_planes}
        groups = {
            across: {mask: swap(start, "ctx", mask) if mask else start for mask in row_columns}
            for across, start in starts.items()
        }
        near_queries = list(groups[0].values()) + list(starts.values())
        far_queries = [pack for group in groups.values() for pack in group.values()]
        index_scores = index_block(after(meta, *near_queries), index_keys, index_query.shape[1], per)

        half = tokens // 2
        pieces, sent, shown = [(0, 0, slab)], [], []
        for across in token_planes[1:]:
            for offset in (0, half):
                piece = slab[:, offset : offset + half]
                sent.append(swap(after(piece, *sent[-1:]), "row", across))
                pieces.append((across, offset, sent[-1]))
        slabs, places = [], []
        for across, offset, piece in pieces:
            for mask in token_columns:
                one = piece
                if mask:
                    late = list(starts.values()) if offset else []
                    one = swap(after(piece, *late, *shown[-1:]), "ctx", mask)
                    shown.append(one)
                for core in (0, 1):
                    if core and mask and offset:
                        one = after(one, index_scores, *far_queries)
                    slabs.append(swap(one, "ctx", 1) if core else one)
                    places.append((core, across, mask, offset))

        parts, last = [], [index_scores]
        split = 2
        some = per // split
        for across in row_planes[1:] + row_planes[:1]:
            mine = []
            for mask in reversed(row_columns):
                pack = after(groups[across][mask], *last)
                sizes = (planes, tokens)
                done = attend([pack], slabs, places, width, sizes, masked, split if across else 1)
                last = list(done)
                first = [] if across else [back[0] for back in parts]
                mine.append([swap(after(a, *first), "ctx", mask) if mask else a for a in done])
            if across:
                back = []
                for i in range(split):
                    rows = range(i * some, (i + 1) * some)
                    mixed = combine([part[i] for part in mine], [rows[0]] * len(mine), rows, heads)
                    back.append(swap(after(mixed, *back), "row", across))
                    last = last + [mixed] if i == 0 else last
                parts.append(back)
            else:
                own = [part[0] for part in mine]
        attended = None
        for i in range(split):
            rows = range(i * some, (i + 1) * some)
            far = [back[i] for back in parts]
            begins = [rows[0]] * len(far) + [0] * len(own)
            cost = TINY if i == split - 1 else LONG
            attended = finish(far + own, begins, rows, per, heads, attended, cost)
        return attended, index_scores

    return jax.shard_map(
        body,
        mesh=mesh,
        in_specs=(
            P(("ctx", "row"), None),
            P("ctx", None),
            P(("row", "ctx"), None, None),
            P(("row", "ctx"), None, None),
            P(("row", "ctx"), None),
            P(("row", "ctx"), None),
        ),
        out_specs=(P(("row", "ctx"), None, None), P("row", "ctx")),
        check_vma=False,
    )
```

```python
import functools

import jax
import jax.numpy as jnp
from jax import lax
from jax.experimental import pallas as pl
from jax.experimental.pallas import tpu as pltpu
from jax.sharding import PartitionSpec as P

LATENT = 512
SCORE_DIM = 192
SEL_MOST = 256
TOK_DEV = 4096
RUN = TOK_DEV // SEL_MOST
LANES = 128
AUX = 16
BATCH = 4
SCALE = SCORE_DIM ** (-0.5) * 1.4426950408889634
VMEM = pltpu.VMEM
LONG = pl.CostEstimate(flops=1000, bytes_accessed=60000000, transcendentals=0)
TINY = pl.CostEstimate(flops=1000, bytes_accessed=1000, transcendentals=0)


def whole_vmem(count):
    return [pl.BlockSpec(memory_space=VMEM)] * count


def params(mib):
    return pltpu.CompilerParams(vmem_limit_bytes=mib * 1024 * 1024)


def near(arrays):
    return [pltpu.with_memory_space_constraint(a, VMEM) for a in arrays]


def table_kernel(query_ref, selected_ref, out_ref):
    rows, width, _ = query_ref.shape
    his = out_ref.shape[1] - width
    picks = selected_ref.shape[1]
    hi_at = lax.broadcasted_iota(jnp.int32, (his, picks), 0)
    lo_at = lax.broadcasted_iota(jnp.int32, (LANES, picks), 0)
    out_ref[:, :width, :] = query_ref[...]
    for row in range(rows):
        token = selected_ref[row : row + 1, :]
        offset = (token % RUN + 1).astype(jnp.float32)
        run = token // RUN
        high = (hi_at == run // LANES).astype(jnp.float32).astype(jnp.bfloat16)
        low = jnp.where(lo_at == run % LANES, offset, 0.0).astype(jnp.bfloat16)
        table = lax.dot_general(
            high, low, (((1,), (1,)), ((), ())), preferred_element_type=jnp.float32
        )
        out_ref[row, width:, :] = table.astype(jnp.bfloat16)


def with_table(query, selected, his):
    rows, width, heads = query.shape
    return pl.pallas_call(
        table_kernel,
        out_shape=jax.ShapeDtypeStruct((rows, width + his, heads), jnp.bfloat16),
        in_specs=whole_vmem(2),
        out_specs=pl.BlockSpec(memory_space=VMEM),
        compiler_params=params(8),
        cost_estimate=TINY,
        name="table",
    )(query, selected)


def three(value):
    first = value.astype(jnp.bfloat16).astype(jnp.float32)
    rest = value - first
    second = rest.astype(jnp.bfloat16).astype(jnp.float32)
    return [first, second, rest - second]


def aux_tile(total, peak):
    pad = jnp.zeros((AUX - 6, LANES), jnp.float32)
    return jnp.concatenate(three(total) + three(peak) + [pad], axis=0).astype(jnp.bfloat16)


def attend_kernel(places, blocks, per, width, sizes, masked, parts, *refs):
    shards = 1 + max(array for array, *_ in places)
    packs, slabs = refs[:blocks], refs[blocks : blocks + shards]
    outs, keys, table = refs[blocks + shards : -2], refs[-2], refs[-1]
    some = per // parts
    rows = blocks * per
    span = RUN * RUN
    here, plane = lax.axis_index("ctx"), lax.axis_index("row")
    planes, tokens = sizes
    for i, pack in enumerate(packs):
        table[i * per : (i + 1) * per] = pack[:, width:, :].astype(jnp.float32)
    spare = [jnp.zeros((-rows % 8, LANES), jnp.float32)] * (rows % 8 > 0)
    lane = lax.broadcasted_iota(jnp.int32, (rows + -rows % 8, LANES), 1)
    base = (lane % RUN * RUN - 1).astype(jnp.float32)
    spread = lax.broadcasted_iota(jnp.int32, (RUN, span), 1).astype(jnp.float32)
    targets, begin = [], 0
    for _, _, count, core, across, mask, offset in places:
        start = ((here ^ mask ^ core) * planes + (plane ^ across)) * (tokens // RUN) + offset // RUN
        row, shift = start // LANES, (LANES - start % LANES + begin) % LANES
        line = [table[i, pl.ds(row, 1), :] for i in range(rows)]
        line = pltpu.roll(jnp.concatenate(line + spare, axis=0), shift, 1)
        tile = line if begin % LANES == 0 else jnp.where(lane >= begin % LANES, line, tile)
        begin += count // RUN
        if begin % LANES == 0:
            targets.append(jnp.transpose(jnp.where(tile > 0.0, base + tile, -1.0)))
    slot = 0
    for array, lanes, count, *_ in places:
        for at in range(lanes, lanes + count, span):
            target = targets[slot // LANES][slot % LANES : slot % LANES + RUN, :]
            hits = [
                (spread == target[:, i : i + 1]).astype(jnp.float32).astype(jnp.bfloat16)
                for i in range(rows)
            ]
            picked = lax.dot_general(
                jnp.concatenate(hits, axis=0),
                slabs[array][:, at : at + span],
                (((1,), (1,)), ((), ())),
                preferred_element_type=jnp.float32,
            ).astype(jnp.bfloat16)
            keys[:, slot : slot + RUN, :] = picked.reshape(rows, RUN, width)
            slot += RUN
    for first in range(0, rows, BATCH):
        group = range(first, min(first + BATCH, rows))
        logits = [
            jnp.dot(
                keys[row],
                packs[row // per][row % per, :width, :],
                preferred_element_type=jnp.float32,
            )
            for row in group
        ]
        done = []
        for row, scores in zip(group, logits):
            if masked:
                known = jnp.concatenate([t[:, row : row + 1] for t in targets], axis=0) >= 0.0
                known = jnp.broadcast_to(known, scores.shape)
                scores = jnp.where(known, scores, -1e30)
            top = jnp.max(scores, axis=0, keepdims=True)
            weights = jnp.exp2((scores - top) * SCALE)
            if masked:
                weights = jnp.where(known, weights, 0.0)
            weights = weights.astype(jnp.bfloat16)
            total = jnp.sum(weights.astype(jnp.float32), axis=0, keepdims=True)
            done.append((weights, total, top * SCALE))
        for row, (weights, total, peak) in zip(group, done):
            block, at = row // per, row % per
            sums = lax.dot_general(
                weights,
                keys[row, :, :LATENT],
                (((0,), (0,)), ((), ())),
                preferred_element_type=jnp.float32,
            )
            heads = sums.shape[0]
            out, at = outs[block * parts + at // some], at % some
            out[at * heads : (at + 1) * heads, :] = sums.astype(jnp.bfloat16)
            out[some * heads :, at * LANES : (at + 1) * LANES] = aux_tile(total, peak)


def attend(packs, slabs, places, width, sizes, masked, parts):
    blocks = len(packs)
    per, tall, heads = packs[0].shape
    slots = sum(count for _, _, count, *_ in places) // RUN
    out = VMEM((per // parts * heads + AUX, LATENT), jnp.bfloat16)
    return pl.pallas_call(
        functools.partial(attend_kernel, places, blocks, per, width, sizes, masked, parts),
        out_shape=[out] * (blocks * parts),
        in_specs=whole_vmem(blocks + len(slabs)),
        out_specs=whole_vmem(blocks * parts),
        scratch_shapes=[
            VMEM((blocks * per, slots, width), jnp.bfloat16),
            VMEM((blocks * per, tall - width, LANES), jnp.float32),
        ],
        compiler_params=params(14),
        cost_estimate=TINY,
        name="attend",
    )(*near(packs), *near(slabs))


def combine_kernel(begins, rows, heads, last, *refs):
    parts, out = refs[: len(begins)], refs[-1]
    for row in rows:
        blocks, totals, peaks = [], [], []
        for ref, begin in zip(parts, begins):
            some, at = (ref.shape[0] - AUX) // heads, row - begin
            aux = ref[some * heads :, at * LANES : (at + 1) * LANES].astype(jnp.float32)
            totals.append(aux[0:1] + aux[1:2] + aux[2:3])
            peaks.append(aux[3:4] + aux[4:5] + aux[5:6])
            blocks.append(ref[at * heads : (at + 1) * heads, :].astype(jnp.float32))
        peak = functools.reduce(jnp.maximum, peaks)
        shares = [jnp.exp2(p - peak) for p in peaks]
        total = functools.reduce(jnp.add, [s * t for s, t in zip(shares, totals)])
        if last:
            shares = [s / total for s in shares]
        pad = -len(shares) % 8
        columns = jnp.transpose(
            jnp.concatenate(shares + [jnp.zeros((pad, LANES), jnp.float32)] * (pad > 0), axis=0)
        )
        terms = [block * columns[:, i : i + 1] for i, block in enumerate(blocks)]
        mixed = functools.reduce(jnp.add, terms).astype(jnp.bfloat16)
        at = row - rows[0]
        if last:
            out[at] = mixed
        else:
            out[at * heads : (at + 1) * heads, :] = mixed
            out[len(rows) * heads :, at * LANES : (at + 1) * LANES] = aux_tile(total, peak)


def combine(parts, begins, rows, heads):
    return pl.pallas_call(
        functools.partial(combine_kernel, begins, rows, heads, False),
        out_shape=VMEM((len(rows) * heads + AUX, LATENT), jnp.bfloat16),
        in_specs=whole_vmem(len(parts)),
        out_specs=pl.BlockSpec(memory_space=VMEM),
        compiler_params=params(8),
        cost_estimate=TINY,
        name="combine",
    )(*near(parts))


def finish(parts, begins, rows, per, heads, done, cost):
    count, at = len(rows), rows[0] // len(rows)
    more = [] if done is None else [done]
    return pl.pallas_call(
        functools.partial(combine_kernel, begins, rows, heads, True),
        grid=(1,),
        out_shape=jax.ShapeDtypeStruct((per, heads, LATENT), jnp.bfloat16),
        in_specs=whole_vmem(len(parts)) + [pl.BlockSpec(memory_space=pl.ANY)] * len(more),
        out_specs=pl.BlockSpec((count, heads, LATENT), lambda i: (at, 0, 0)),
        input_output_aliases={len(parts): 0} if more else {},
        compiler_params=params(8),
        cost_estimate=cost,
        name="finish",
    )(*near(parts), *more)


def index_kernel(heads, per, masks, meta_ref, keys_ref, out_ref, gate_scr):
    rows = meta_ref.shape[0]
    tokens = keys_ref.shape[0]

    @pl.when(pl.program_id(0) == 0)
    def _():
        for first in range(0, rows, 8):
            lines = jnp.concatenate(
                [meta_ref[first + i, heads : heads + 8, :].astype(jnp.float32)[:1] for i in range(8)],
                axis=0,
            )
            turned = jnp.transpose(lines)
            for i in range(8):
                gate_scr[first + i] = jnp.broadcast_to(turned[:heads, i : i + 1], (heads, LANES))

    for first in range(0, rows, 2 * per):
        queries = jnp.concatenate([meta_ref[first + i, :heads, :] for i in range(2 * per)], axis=0)
        logits = lax.dot_general(
            queries, keys_ref[...], (((1,), (1,)), ((), ())), preferred_element_type=jnp.float32
        )
        lines = []
        for i in range(2 * per):
            gate = jnp.concatenate([gate_scr[first + i]] * (tokens // LANES), axis=1)
            terms = jnp.maximum(logits[i * heads : (i + 1) * heads, :], 0.0) * gate
            lines.append(jnp.sum(terms, axis=0, keepdims=True))
        here = lax.axis_index("ctx")
        ours, mates = lines[:per], lines[per:]
        group = jnp.where(
            here % 2 == 0, jnp.concatenate(ours + mates, axis=0), jnp.concatenate(mates + ours, axis=0)
        )
        place = (here ^ masks[first // (2 * per)]) // 2
        out_ref[pl.ds(pl.multiple_of(place * 2 * per, 2 * per), 2 * per), :] = group


def index_block(meta, index_keys, heads, per, masks):
    rows, tall, size = meta.shape
    tokens = index_keys.shape[0]
    block = 512
    return pl.pallas_call(
        functools.partial(index_kernel, heads, per, masks),
        grid=(tokens // block,),
        out_shape=jax.ShapeDtypeStruct((rows, tokens), jnp.float32),
        in_specs=[
            pl.BlockSpec((rows, tall, size), lambda i: (0, 0, 0)),
            pl.BlockSpec((block, size), lambda i: (i, 0)),
        ],
        out_specs=pl.BlockSpec((rows, block), lambda i: (0, i)),
        scratch_shapes=[VMEM((rows, heads, LANES), jnp.float32)],
        compiler_params=params(14),
        cost_estimate=TINY,
        name="index",
    )(meta, index_keys)


def solution(mesh):
    columns, planes = mesh.shape["ctx"], mesh.shape["row"]
    token_columns = [0, 2] if columns > 2 else [0]
    token_planes = [0, 1] if planes > 1 else [0]
    row_columns = list(range(0, columns, 4))
    row_planes = list(range(0, planes, 2))

    def swap(array, axis, mask):
        size = mesh.shape[axis]
        return lax.ppermute(array, axis, [(i, i ^ mask) for i in range(size)])

    def body(latent_cache, index_keys, query_latent, index_query, index_gates, selected):
        per, _, width = query_latent.shape
        heads = query_latent.shape[1]
        tokens = latent_cache.shape[0]
        runs = tokens // RUN
        all_runs = runs * columns * planes
        masked = all_runs != selected.shape[1]
        slab = jnp.swapaxes(latent_cache, 0, 1)
        query = jnp.swapaxes(query_latent, 1, 2)

        def after(array, *others):
            return lax.optimization_barrier((array, *others))[0]

        gate_rows = jnp.pad(
            index_gates[:, None, :], ((0, 0), (0, AUX - 1), (0, LANES - index_gates.shape[1]))
        )
        meta = jnp.concatenate([index_query, gate_rows], axis=1)
        meta = jnp.concatenate([meta, swap(meta, "ctx", 1)])

        packed = with_table(query, selected, all_runs // LANES)
        starts = {across: swap(packed, "row", across) if across else packed for across in row_planes}
        groups = {
            across: {mask: swap(start, "ctx", mask) if mask else start for mask in row_columns}
            for across, start in starts.items()
        }
        far_queries = [pack for group in groups.values() for pack in group.values()]
        half, quarter = tokens // 2, tokens // 4
        pieces, sent, shown = [(0, 0, slab)], [], []
        for across in token_planes[1:]:
            for offset, count in ((0, half), (half, quarter)):
                piece = slab[:, offset : offset + count]
                sent.append(swap(after(piece, *sent[-1:]), "row", across))
                pieces.append((across, offset, sent[-1]))
        slabs, places = [], []
        for across, offset, piece in pieces:
            for mask in token_columns:
                one = piece
                if mask:
                    late = list(starts.values()) if offset else []
                    one = swap(after(piece, *late, *shown[-1:]), "ctx", mask)
                    shown.append(one)
                for core in (0, 1):
                    if core and mask and offset:
                        one = after(one, *far_queries)
                    places.append((len(slabs), 0, piece.shape[1], core, across, mask, offset))
                    slabs.append(swap(one, "ctx", 1) if core else one)
        for across in token_planes[1:]:
            first = half + quarter
            both = [held[:, first:] for held in (slab, *shown[:1])]
            both = swap(jnp.concatenate(both, axis=1), "row", across)
            for core in (0, 1):
                for i, mask in enumerate(token_columns):
                    places.append((len(slabs), i * quarter, quarter, core, across, mask, first))
                slabs.append(swap(both, "ctx", 1) if core else both)

        masks = [0]
        for bit in [1 << k for k in range(2, columns.bit_length() - 1)] + token_columns[1:]:
            meta = after(meta, *(shown[-1:] if bit in token_columns else far_queries))
            meta = jnp.concatenate([meta, swap(meta, "ctx", bit)])
            masks += [mask ^ bit for mask in masks]

        parts, last = [], []
        split = 2
        some = per // split
        for across in row_planes[1:] + row_planes[:1]:
            mine = []
            for mask in reversed(row_columns):
                pack = after(groups[across][mask], *last) if last else groups[across][mask]
                sizes = (planes, tokens)
                done = attend([pack], slabs, places, width, sizes, masked, split if across else 1)
                last = list(done)
                first = [] if across else [back[0] for back in parts]
                mine.append([swap(after(a, *first), "ctx", mask) if mask else a for a in done])
            if across:
                back = []
                for i in range(split):
                    rows = range(i * some, (i + 1) * some)
                    mixed = combine([part[i] for part in mine], [rows[0]] * len(mine), rows, heads)
                    back.append(swap(mixed, "row", across))
                    last = last + [mixed, meta] if i == 0 else last
                parts.append(back)
            else:
                own = [part[0] for part in mine]
        index_scores = index_block(after(meta, *last), index_keys, index_query.shape[1], per, masks)
        attended = None
        for i in range(split):
            rows = range(i * some, (i + 1) * some)
            far = [back[i] for back in parts]
            begins = [rows[0]] * len(far) + [0] * len(own)
            cost = TINY if i == split - 1 else LONG
            attended = finish(far + own, begins, rows, per, heads, attended, cost)
        return attended, index_scores

    return jax.shard_map(
        body,
        mesh=mesh,
        in_specs=(
            P(("ctx", "row"), None),
            P("ctx", None),
            P(("row", "ctx"), None, None),
            P(("row", "ctx"), None, None),
            P(("row", "ctx"), None),
            P(("row", "ctx"), None),
        ),
        out_specs=(P(("row", "ctx"), None, None), P("row", "ctx")),
        check_vma=False,
    )
```

```python
import functools

import jax
import jax.numpy as jnp
from jax import lax
from jax.experimental import pallas as pl
from jax.experimental.pallas import tpu as pltpu
from jax.sharding import PartitionSpec as P

LATENT = 512
SCORE_DIM = 192
SEL_MOST = 256
TOK_DEV = 4096
RUN = TOK_DEV // SEL_MOST
LANES = 128
AUX = 16
BATCH = 4
SCALE = SCORE_DIM ** (-0.5) * 1.4426950408889634
VMEM = pltpu.VMEM
LONG = pl.CostEstimate(flops=1000, bytes_accessed=60000000, transcendentals=0)
TINY = pl.CostEstimate(flops=1000, bytes_accessed=1000, transcendentals=0)


def whole_vmem(count):
    return [pl.BlockSpec(memory_space=VMEM)] * count


def params(mib):
    return pltpu.CompilerParams(vmem_limit_bytes=mib * 1024 * 1024)


def near(arrays):
    return [pltpu.with_memory_space_constraint(a, VMEM) for a in arrays]


def table_kernel(query_ref, selected_ref, out_ref):
    rows, width, _ = query_ref.shape
    his = out_ref.shape[1] - width
    picks = selected_ref.shape[1]
    hi_at = lax.broadcasted_iota(jnp.int32, (his, picks), 0)
    lo_at = lax.broadcasted_iota(jnp.int32, (LANES, picks), 0)
    out_ref[:, :width, :] = query_ref[...]
    for row in range(rows):
        token = selected_ref[row : row + 1, :]
        offset = (token % RUN + 1).astype(jnp.float32)
        run = token // RUN
        high = (hi_at == run // LANES).astype(jnp.float32).astype(jnp.bfloat16)
        low = jnp.where(lo_at == run % LANES, offset, 0.0).astype(jnp.bfloat16)
        table = lax.dot_general(
            high, low, (((1,), (1,)), ((), ())), preferred_element_type=jnp.float32
        )
        out_ref[row, width:, :] = table.astype(jnp.bfloat16)


def with_table(query, selected, his):
    rows, width, heads = query.shape
    return pl.pallas_call(
        table_kernel,
        out_shape=jax.ShapeDtypeStruct((rows, width + his, heads), jnp.bfloat16),
        in_specs=whole_vmem(2),
        out_specs=pl.BlockSpec(memory_space=VMEM),
        compiler_params=params(8),
        cost_estimate=TINY,
        name="table",
    )(query, selected)


def three(value):
    first = value.astype(jnp.bfloat16).astype(jnp.float32)
    rest = value - first
    second = rest.astype(jnp.bfloat16).astype(jnp.float32)
    return [first, second, rest - second]


def aux_tile(total, peak):
    pad = jnp.zeros((AUX - 6, LANES), jnp.float32)
    return jnp.concatenate(three(total) + three(peak) + [pad], axis=0).astype(jnp.bfloat16)


def attend_kernel(places, blocks, per, width, sizes, masked, parts, *refs):
    shards = 1 + max(array for array, *_ in places)
    packs, slabs = refs[:blocks], refs[blocks : blocks + shards]
    outs, keys, table = refs[blocks + shards : -2], refs[-2], refs[-1]
    some = per // parts
    rows = blocks * per
    span = RUN * RUN
    here, plane = lax.axis_index("ctx"), lax.axis_index("row")
    planes, tokens = sizes
    for i, pack in enumerate(packs):
        table[i * per : (i + 1) * per] = pack[:, width:, :].astype(jnp.float32)
    spare = [jnp.zeros((-rows % 8, LANES), jnp.float32)] * (rows % 8 > 0)
    lane = lax.broadcasted_iota(jnp.int32, (rows + -rows % 8, LANES), 1)
    base = (lane % RUN * RUN - 1).astype(jnp.float32)
    spread = lax.broadcasted_iota(jnp.int32, (RUN, span), 1).astype(jnp.float32)
    targets, begin = [], 0
    for _, _, count, core, across, mask, offset in places:
        start = ((here ^ mask ^ core) * planes + (plane ^ across)) * (tokens // RUN) + offset // RUN
        row, shift = start // LANES, (LANES - start % LANES + begin) % LANES
        line = [table[i, pl.ds(row, 1), :] for i in range(rows)]
        line = pltpu.roll(jnp.concatenate(line + spare, axis=0), shift, 1)
        tile = line if begin % LANES == 0 else jnp.where(lane >= begin % LANES, line, tile)
        begin += count // RUN
        if begin % LANES == 0:
            targets.append(jnp.transpose(jnp.where(tile > 0.0, base + tile, -1.0)))
    slot = 0
    for array, lanes, count, *_ in places:
        for at in range(lanes, lanes + count, span):
            target = targets[slot // LANES][slot % LANES : slot % LANES + RUN, :]
            hits = [
                (spread == target[:, i : i + 1]).astype(jnp.float32).astype(jnp.bfloat16)
                for i in range(rows)
            ]
            picked = lax.dot_general(
                jnp.concatenate(hits, axis=0),
                slabs[array][:, at : at + span],
                (((1,), (1,)), ((), ())),
                preferred_element_type=jnp.float32,
            ).astype(jnp.bfloat16)
            keys[:, slot : slot + RUN, :] = picked.reshape(rows, RUN, width)
            slot += RUN
    for first in range(0, rows, BATCH):
        group = range(first, min(first + BATCH, rows))
        logits = [
            jnp.dot(
                keys[row],
                packs[row // per][row % per, :width, :],
                preferred_element_type=jnp.float32,
            )
            for row in group
        ]
        done = []
        for row, scores in zip(group, logits):
            if masked:
                known = jnp.concatenate([t[:, row : row + 1] for t in targets], axis=0) >= 0.0
                known = jnp.broadcast_to(known, scores.shape)
                scores = jnp.where(known, scores, -1e30)
            top = jnp.max(scores, axis=0, keepdims=True)
            weights = jnp.exp2((scores - top) * SCALE)
            if masked:
                weights = jnp.where(known, weights, 0.0)
            weights = weights.astype(jnp.bfloat16)
            total = jnp.sum(weights.astype(jnp.float32), axis=0, keepdims=True)
            done.append((weights, total, top * SCALE))
        for row, (weights, total, peak) in zip(group, done):
            block, at = row // per, row % per
            sums = lax.dot_general(
                weights,
                keys[row, :, :LATENT],
                (((0,), (0,)), ((), ())),
                preferred_element_type=jnp.float32,
            )
            heads = sums.shape[0]
            out, at = outs[block * parts + at // some], at % some
            out[at * heads : (at + 1) * heads, :] = sums.astype(jnp.bfloat16)
            out[some * heads :, at * LANES : (at + 1) * LANES] = aux_tile(total, peak)


def attend(packs, slabs, places, width, sizes, masked, parts):
    blocks = len(packs)
    per, tall, heads = packs[0].shape
    slots = sum(count for _, _, count, *_ in places) // RUN
    out = VMEM((per // parts * heads + AUX, LATENT), jnp.bfloat16)
    return pl.pallas_call(
        functools.partial(attend_kernel, places, blocks, per, width, sizes, masked, parts),
        out_shape=[out] * (blocks * parts),
        in_specs=whole_vmem(blocks + len(slabs)),
        out_specs=whole_vmem(blocks * parts),
        scratch_shapes=[
            VMEM((blocks * per, slots, width), jnp.bfloat16),
            VMEM((blocks * per, tall - width, LANES), jnp.float32),
        ],
        compiler_params=params(14),
        cost_estimate=TINY,
        name="attend",
    )(*near(packs), *near(slabs))


def combine_kernel(begins, rows, heads, last, *refs):
    parts, out = refs[: len(begins)], refs[-1]
    for row in rows:
        blocks, totals, peaks = [], [], []
        for ref, begin in zip(parts, begins):
            some, at = (ref.shape[0] - AUX) // heads, row - begin
            aux = ref[some * heads :, at * LANES : (at + 1) * LANES].astype(jnp.float32)
            totals.append(aux[0:1] + aux[1:2] + aux[2:3])
            peaks.append(aux[3:4] + aux[4:5] + aux[5:6])
            blocks.append(ref[at * heads : (at + 1) * heads, :].astype(jnp.float32))
        peak = functools.reduce(jnp.maximum, peaks)
        shares = [jnp.exp2(p - peak) for p in peaks]
        total = functools.reduce(jnp.add, [s * t for s, t in zip(shares, totals)])
        if last:
            shares = [s / total for s in shares]
        pad = -len(shares) % 8
        columns = jnp.transpose(
            jnp.concatenate(shares + [jnp.zeros((pad, LANES), jnp.float32)] * (pad > 0), axis=0)
        )
        terms = [block * columns[:, i : i + 1] for i, block in enumerate(blocks)]
        mixed = functools.reduce(jnp.add, terms).astype(jnp.bfloat16)
        at = row - rows[0]
        if last:
            out[at] = mixed
        else:
            out[at * heads : (at + 1) * heads, :] = mixed
            out[len(rows) * heads :, at * LANES : (at + 1) * LANES] = aux_tile(total, peak)


def combine(parts, begins, rows, heads):
    return pl.pallas_call(
        functools.partial(combine_kernel, begins, rows, heads, False),
        out_shape=VMEM((len(rows) * heads + AUX, LATENT), jnp.bfloat16),
        in_specs=whole_vmem(len(parts)),
        out_specs=pl.BlockSpec(memory_space=VMEM),
        compiler_params=params(8),
        cost_estimate=TINY,
        name="combine",
    )(*near(parts))


def finish(parts, begins, rows, per, heads, done, cost):
    count, at = len(rows), rows[0] // len(rows)
    more = [] if done is None else [done]
    return pl.pallas_call(
        functools.partial(combine_kernel, begins, rows, heads, True),
        grid=(1,),
        out_shape=jax.ShapeDtypeStruct((per, heads, LATENT), jnp.bfloat16),
        in_specs=whole_vmem(len(parts)) + [pl.BlockSpec(memory_space=pl.ANY)] * len(more),
        out_specs=pl.BlockSpec((count, heads, LATENT), lambda i: (at, 0, 0)),
        input_output_aliases={len(parts): 0} if more else {},
        compiler_params=params(8),
        cost_estimate=cost,
        name="finish",
    )(*near(parts), *more)


def index_kernel(heads, per, masks, meta_ref, keys_ref, out_ref, gate_scr):
    rows = meta_ref.shape[0]
    tokens = keys_ref.shape[0]

    @pl.when(pl.program_id(0) == 0)
    def _():
        for first in range(0, rows, 8):
            lines = jnp.concatenate(
                [meta_ref[first + i, heads : heads + AUX, :].astype(jnp.float32)[:1] for i in range(8)],
                axis=0,
            )
            turned = jnp.transpose(lines)
            for i in range(8):
                gate_scr[first + i] = jnp.broadcast_to(turned[:heads, i : i + 1], (heads, LANES))

    for first in range(0, rows, 2 * per):
        queries = jnp.concatenate([meta_ref[first + i, :heads, :] for i in range(2 * per)], axis=0)
        logits = lax.dot_general(
            queries, keys_ref[...], (((1,), (1,)), ((), ())), preferred_element_type=jnp.float32
        )
        lines = []
        for i in range(2 * per):
            gate = jnp.concatenate([gate_scr[first + i]] * (tokens // LANES), axis=1)
            terms = jnp.maximum(logits[i * heads : (i + 1) * heads, :], 0.0) * gate
            lines.append(jnp.sum(terms, axis=0, keepdims=True))
        here = lax.axis_index("ctx")
        ours, mates = lines[:per], lines[per:]
        group = jnp.where(
            here % 2 == 0, jnp.concatenate(ours + mates, axis=0), jnp.concatenate(mates + ours, axis=0)
        )
        place = (here ^ masks[first // (2 * per)]) // 2
        out_ref[pl.ds(pl.multiple_of(place * 2 * per, 2 * per), 2 * per), :] = group


def index_block(meta, index_keys, heads, per, masks):
    rows, tall, size = meta.shape
    tokens = index_keys.shape[0]
    block = 512
    return pl.pallas_call(
        functools.partial(index_kernel, heads, per, masks),
        grid=(tokens // block,),
        out_shape=jax.ShapeDtypeStruct((rows, tokens), jnp.float32),
        in_specs=[
            pl.BlockSpec((rows, tall, size), lambda i: (0, 0, 0)),
            pl.BlockSpec((block, size), lambda i: (i, 0)),
        ],
        out_specs=pl.BlockSpec((rows, block), lambda i: (0, i)),
        scratch_shapes=[VMEM((rows, heads, LANES), jnp.float32)],
        compiler_params=params(14),
        cost_estimate=TINY,
        name="index",
    )(meta, index_keys)


def solution(mesh):
    columns, planes = mesh.shape["ctx"], mesh.shape["row"]
    token_columns = [0, 2] if columns > 2 else [0]
    token_planes = [0, 1] if planes > 1 else [0]
    row_columns = list(range(0, columns, 4))
    row_planes = list(range(0, planes, 2))

    def swap(array, axis, mask):
        size = mesh.shape[axis]
        return lax.ppermute(array, axis, [(i, i ^ mask) for i in range(size)])

    def body(latent_cache, index_keys, query_latent, index_query, index_gates, selected):
        per, _, width = query_latent.shape
        heads = query_latent.shape[1]
        tokens = latent_cache.shape[0]
        runs = tokens // RUN
        all_runs = runs * columns * planes
        masked = all_runs != selected.shape[1]
        slab = jnp.swapaxes(latent_cache, 0, 1)
        query = jnp.swapaxes(query_latent, 1, 2)

        def after(array, *others):
            return lax.optimization_barrier((array, *others))[0]

        gate_rows = jnp.pad(
            index_gates[:, None, :], ((0, 0), (0, AUX - 1), (0, LANES - index_gates.shape[1]))
        )
        meta = jnp.concatenate([index_query, gate_rows], axis=1)
        meta = jnp.concatenate([meta, swap(meta, "ctx", 1)])

        packed = with_table(query, selected, all_runs // LANES)
        starts = {across: swap(packed, "row", across) if across else packed for across in row_planes}
        groups = {
            across: {mask: swap(start, "ctx", mask) if mask else start for mask in row_columns}
            for across, start in starts.items()
        }
        far_queries = [pack for group in groups.values() for pack in group.values()]
        half, quarter = tokens // 2, tokens // 4
        pieces, sent, shown = [(0, 0, slab)], [], []
        for across in token_planes[1:]:
            for offset, count in ((0, half), (half, quarter)):
                piece = slab[:, offset : offset + count]
                sent.append(swap(after(piece, *sent[-1:]), "row", across))
                pieces.append((across, offset, sent[-1]))
        slabs, places = [], []
        for across, offset, piece in pieces:
            for mask in token_columns:
                one = piece
                if mask:
                    late = list(starts.values()) if offset else []
                    one = swap(after(piece, *late, *shown[-1:]), "ctx", mask)
                    shown.append(one)
                for core in (0, 1):
                    if core and mask and offset:
                        one = after(one, *far_queries)
                    places.append((len(slabs), 0, piece.shape[1], core, across, mask, offset))
                    slabs.append(swap(one, "ctx", 1) if core else one)
        for across in token_planes[1:]:
            first = half + quarter
            both = [held[:, first:] for held in (slab, *shown[:1])]
            both = swap(jnp.concatenate(both, axis=1), "row", across)
            for core in (0, 1):
                for i, mask in enumerate(token_columns):
                    places.append((len(slabs), i * quarter, quarter, core, across, mask, first))
                slabs.append(swap(both, "ctx", 1) if core else both)

        masks = [0]
        for bit in [1 << k for k in range(2, columns.bit_length() - 1)] + token_columns[1:]:
            meta = after(meta, *(shown[-1:] if bit in token_columns else far_queries))
            meta = jnp.concatenate([meta, swap(meta, "ctx", bit)])
            masks += [mask ^ bit for mask in masks]

        parts, last = [], []
        split = 2
        some = per // split
        for across in row_planes[1:] + row_planes[:1]:
            mine = []
            for mask in reversed(row_columns):
                pack = after(groups[across][mask], *last) if last else groups[across][mask]
                sizes = (planes, tokens)
                done = attend([pack], slabs, places, width, sizes, masked, split if across else 1)
                last = list(done)
                first = [] if across else [back[0] for back in parts]
                mine.append([swap(after(a, *first), "ctx", mask) if mask else a for a in done])
            if across:
                back = []
                for i in range(split):
                    rows = range(i * some, (i + 1) * some)
                    mixed = combine([part[i] for part in mine], [rows[0]] * len(mine), rows, heads)
                    back.append(swap(mixed, "row", across))
                    last = last + [mixed, meta] if i == 0 else last
                parts.append(back)
            else:
                own = [part[0] for part in mine]
        index_scores = index_block(after(meta, *last), index_keys, index_query.shape[1], per, masks)
        attended = None
        for i in range(split):
            rows = range(i * some, (i + 1) * some)
            far = [back[i] for back in parts]
            begins = [rows[0]] * len(far) + [0] * len(own)
            cost = TINY if i == split - 1 else LONG
            attended = finish(far + own, begins, rows, per, heads, attended, cost)
        return attended, index_scores

    return jax.shard_map(
        body,
        mesh=mesh,
        in_specs=(
            P(("ctx", "row"), None),
            P("ctx", None),
            P(("row", "ctx"), None, None),
            P(("row", "ctx"), None, None),
            P(("row", "ctx"), None),
            P(("row", "ctx"), None),
        ),
        out_specs=(P(("row", "ctx"), None, None), P("row", "ctx")),
        check_vma=False,
    )
```

```python
import functools

import jax
import jax.numpy as jnp
from jax import lax
from jax.experimental import pallas as pl
from jax.experimental.pallas import tpu as pltpu
from jax.sharding import PartitionSpec as P

LATENT = 512
SCORE_DIM = 192
SEL_MOST = 256
TOK_DEV = 4096
RUN = TOK_DEV // SEL_MOST
LANES = 128
AUX = 16
BATCH = 4
SCALE = SCORE_DIM ** (-0.5) * 1.4426950408889634
VMEM = pltpu.VMEM
LONG = pl.CostEstimate(flops=1000, bytes_accessed=60000000, transcendentals=0)
TINY = pl.CostEstimate(flops=1000, bytes_accessed=1000, transcendentals=0)


def whole_vmem(count):
    return [pl.BlockSpec(memory_space=VMEM)] * count


def params(mib):
    return pltpu.CompilerParams(vmem_limit_bytes=mib * 1024 * 1024)


def near(arrays):
    return [pltpu.with_memory_space_constraint(a, VMEM) for a in arrays]


def table_kernel(query_ref, selected_ref, out_ref):
    rows, width, _ = query_ref.shape
    his = out_ref.shape[1] - width
    picks = selected_ref.shape[1]
    hi_at = lax.broadcasted_iota(jnp.int32, (his, picks), 0)
    lo_at = lax.broadcasted_iota(jnp.int32, (LANES, picks), 0)
    out_ref[:, :width, :] = query_ref[...]
    for row in range(rows):
        token = selected_ref[row : row + 1, :]
        offset = (token % RUN + 1).astype(jnp.float32)
        run = token // RUN
        high = (hi_at == run // LANES).astype(jnp.float32).astype(jnp.bfloat16)
        low = jnp.where(lo_at == run % LANES, offset, 0.0).astype(jnp.bfloat16)
        table = lax.dot_general(
            high, low, (((1,), (1,)), ((), ())), preferred_element_type=jnp.float32
        )
        out_ref[row, width:, :] = table.astype(jnp.bfloat16)


def with_table(query, selected, his):
    rows, width, heads = query.shape
    return pl.pallas_call(
        table_kernel,
        out_shape=jax.ShapeDtypeStruct((rows, width + his, heads), jnp.bfloat16),
        in_specs=whole_vmem(2),
        out_specs=pl.BlockSpec(memory_space=VMEM),
        compiler_params=params(8),
        cost_estimate=TINY,
        name="table",
    )(query, selected)


def three(value):
    first = value.astype(jnp.bfloat16).astype(jnp.float32)
    rest = value - first
    second = rest.astype(jnp.bfloat16).astype(jnp.float32)
    return [first, second, rest - second]


def aux_tile(total, peak):
    pad = jnp.zeros((AUX - 6, LANES), jnp.float32)
    return jnp.concatenate(three(total) + three(peak) + [pad], axis=0).astype(jnp.bfloat16)


def attend_kernel(places, blocks, per, width, sizes, masked, parts, *refs):
    shards = 1 + max(array for array, *_ in places)
    packs, slabs = refs[:blocks], refs[blocks : blocks + shards]
    outs, keys, table = refs[blocks + shards : -2], refs[-2], refs[-1]
    some = per // parts
    rows = blocks * per
    span = RUN * RUN
    here, plane = lax.axis_index("ctx"), lax.axis_index("row")
    planes, tokens = sizes
    for i, pack in enumerate(packs):
        table[i * per : (i + 1) * per] = pack[:, width:, :].astype(jnp.float32)
    spare = [jnp.zeros((-rows % 8, LANES), jnp.float32)] * (rows % 8 > 0)
    lane = lax.broadcasted_iota(jnp.int32, (rows + -rows % 8, LANES), 1)
    base = (lane % RUN * RUN - 1).astype(jnp.float32)
    spread = lax.broadcasted_iota(jnp.int32, (RUN, span), 1).astype(jnp.float32)
    targets, begin = [], 0
    for _, _, count, core, across, mask, offset in places:
        start = ((here ^ mask ^ core) * planes + (plane ^ across)) * (tokens // RUN) + offset // RUN
        row, shift = start // LANES, (LANES - start % LANES + begin) % LANES
        line = [table[i, pl.ds(row, 1), :] for i in range(rows)]
        line = pltpu.roll(jnp.concatenate(line + spare, axis=0), shift, 1)
        tile = line if begin % LANES == 0 else jnp.where(lane >= begin % LANES, line, tile)
        begin += count // RUN
        if begin % LANES == 0:
            targets.append(jnp.transpose(jnp.where(tile > 0.0, base + tile, -1.0)))
    slot = 0
    for array, lanes, count, *_ in places:
        for at in range(lanes, lanes + count, span):
            target = targets[slot // LANES][slot % LANES : slot % LANES + RUN, :]
            hits = [
                (spread == target[:, i : i + 1]).astype(jnp.float32).astype(jnp.bfloat16)
                for i in range(rows)
            ]
            picked = lax.dot_general(
                jnp.concatenate(hits, axis=0),
                slabs[array][:, at : at + span],
                (((1,), (1,)), ((), ())),
                preferred_element_type=jnp.float32,
            ).astype(jnp.bfloat16)
            keys[:, slot : slot + RUN, :] = picked.reshape(rows, RUN, width)
            slot += RUN
    for first in range(0, rows, BATCH):
        group = range(first, min(first + BATCH, rows))
        logits = [
            jnp.dot(
                keys[row],
                packs[row // per][row % per, :width, :],
                preferred_element_type=jnp.float32,
            )
            for row in group
        ]
        done = []
        for row, scores in zip(group, logits):
            if masked:
                known = jnp.concatenate([t[:, row : row + 1] for t in targets], axis=0) >= 0.0
                known = jnp.broadcast_to(known, scores.shape)
                scores = jnp.where(known, scores, -1e30)
            top = jnp.max(scores, axis=0, keepdims=True)
            weights = jnp.exp2((scores - top) * SCALE)
            if masked:
                weights = jnp.where(known, weights, 0.0)
            weights = weights.astype(jnp.bfloat16)
            total = jnp.sum(weights.astype(jnp.float32), axis=0, keepdims=True)
            done.append((weights, total, top * SCALE))
        for row, (weights, total, peak) in zip(group, done):
            block, at = row // per, row % per
            sums = lax.dot_general(
                weights,
                keys[row, :, :LATENT],
                (((0,), (0,)), ((), ())),
                preferred_element_type=jnp.float32,
            )
            heads = sums.shape[0]
            out, at = outs[block * parts + at // some], at % some
            out[at * heads : (at + 1) * heads, :] = sums.astype(jnp.bfloat16)
            out[some * heads :, at * LANES : (at + 1) * LANES] = aux_tile(total, peak)


def attend(packs, slabs, places, width, sizes, masked, parts):
    blocks = len(packs)
    per, tall, heads = packs[0].shape
    slots = sum(count for _, _, count, *_ in places) // RUN
    out = VMEM((per // parts * heads + AUX, LATENT), jnp.bfloat16)
    return pl.pallas_call(
        functools.partial(attend_kernel, places, blocks, per, width, sizes, masked, parts),
        out_shape=[out] * (blocks * parts),
        in_specs=whole_vmem(blocks + len(slabs)),
        out_specs=whole_vmem(blocks * parts),
        scratch_shapes=[
            VMEM((blocks * per, slots, width), jnp.bfloat16),
            VMEM((blocks * per, tall - width, LANES), jnp.float32),
        ],
        compiler_params=params(14),
        cost_estimate=TINY,
        name="attend",
    )(*near(packs), *near(slabs))


def combine_kernel(begins, rows, heads, last, *refs):
    parts, out = refs[: len(begins)], refs[-1]
    for row in rows:
        blocks, totals, peaks = [], [], []
        for ref, begin in zip(parts, begins):
            some, at = (ref.shape[0] - AUX) // heads, row - begin
            aux = ref[some * heads :, at * LANES : (at + 1) * LANES].astype(jnp.float32)
            totals.append(aux[0:1] + aux[1:2] + aux[2:3])
            peaks.append(aux[3:4] + aux[4:5] + aux[5:6])
            blocks.append(ref[at * heads : (at + 1) * heads, :].astype(jnp.float32))
        peak = functools.reduce(jnp.maximum, peaks)
        shares = [jnp.exp2(p - peak) for p in peaks]
        total = functools.reduce(jnp.add, [s * t for s, t in zip(shares, totals)])
        if last:
            shares = [s / total for s in shares]
        pad = -len(shares) % 8
        columns = jnp.transpose(
            jnp.concatenate(shares + [jnp.zeros((pad, LANES), jnp.float32)] * (pad > 0), axis=0)
        )
        terms = [block * columns[:, i : i + 1] for i, block in enumerate(blocks)]
        mixed = functools.reduce(jnp.add, terms).astype(jnp.bfloat16)
        at = row - rows[0]
        if last:
            out[at] = mixed
        else:
            out[at * heads : (at + 1) * heads, :] = mixed
            out[len(rows) * heads :, at * LANES : (at + 1) * LANES] = aux_tile(total, peak)


def combine(parts, begins, rows, heads):
    return pl.pallas_call(
        functools.partial(combine_kernel, begins, rows, heads, False),
        out_shape=VMEM((len(rows) * heads + AUX, LATENT), jnp.bfloat16),
        in_specs=whole_vmem(len(parts)),
        out_specs=pl.BlockSpec(memory_space=VMEM),
        compiler_params=params(8),
        cost_estimate=TINY,
        name="combine",
    )(*near(parts))


def finish(parts, begins, rows, per, heads, done, cost):
    count, at = len(rows), rows[0] // len(rows)
    more = [] if done is None else [done]
    return pl.pallas_call(
        functools.partial(combine_kernel, begins, rows, heads, True),
        grid=(1,),
        out_shape=jax.ShapeDtypeStruct((per, heads, LATENT), jnp.bfloat16),
        in_specs=whole_vmem(len(parts)) + [pl.BlockSpec(memory_space=pl.ANY)] * len(more),
        out_specs=pl.BlockSpec((count, heads, LATENT), lambda i: (at, 0, 0)),
        input_output_aliases={len(parts): 0} if more else {},
        compiler_params=params(8),
        cost_estimate=cost,
        name="finish",
    )(*near(parts), *more)


def index_kernel(heads, per, masks, meta_ref, keys_ref, out_ref, gate_scr):
    rows = meta_ref.shape[0]
    tokens = keys_ref.shape[0]

    @pl.when(pl.program_id(0) == 0)
    def _():
        for first in range(0, rows, 8):
            lines = jnp.concatenate(
                [meta_ref[first + i, heads : heads + AUX, :].astype(jnp.float32)[:1] for i in range(8)],
                axis=0,
            )
            turned = jnp.transpose(lines)
            for i in range(8):
                gate_scr[first + i] = jnp.broadcast_to(turned[:heads, i : i + 1], (heads, LANES))

    for first in range(0, rows, 2 * per):
        queries = jnp.concatenate([meta_ref[first + i, :heads, :] for i in range(2 * per)], axis=0)
        logits = lax.dot_general(
            queries, keys_ref[...], (((1,), (1,)), ((), ())), preferred_element_type=jnp.float32
        )
        lines = []
        for i in range(2 * per):
            gate = jnp.concatenate([gate_scr[first + i]] * (tokens // LANES), axis=1)
            terms = jnp.maximum(logits[i * heads : (i + 1) * heads, :], 0.0) * gate
            lines.append(jnp.sum(terms, axis=0, keepdims=True))
        here = lax.axis_index("ctx")
        ours, mates = lines[:per], lines[per:]
        group = jnp.where(
            here % 2 == 0, jnp.concatenate(ours + mates, axis=0), jnp.concatenate(mates + ours, axis=0)
        )
        place = (here ^ masks[first // (2 * per)]) // 2
        out_ref[pl.ds(pl.multiple_of(place * 2 * per, 2 * per), 2 * per), :] = group


def index_block(meta, index_keys, heads, per, masks):
    rows, tall, size = meta.shape
    tokens = index_keys.shape[0]
    block = 512
    return pl.pallas_call(
        functools.partial(index_kernel, heads, per, masks),
        grid=(tokens // block,),
        out_shape=jax.ShapeDtypeStruct((rows, tokens), jnp.float32),
        in_specs=[
            pl.BlockSpec((rows, tall, size), lambda i: (0, 0, 0)),
            pl.BlockSpec((block, size), lambda i: (i, 0)),
        ],
        out_specs=pl.BlockSpec((rows, block), lambda i: (0, i)),
        scratch_shapes=[VMEM((rows, heads, LANES), jnp.float32)],
        compiler_params=params(14),
        cost_estimate=TINY,
        name="index",
    )(meta, index_keys)


def solution(mesh):
    columns, planes = mesh.shape["ctx"], mesh.shape["row"]
    token_columns = [0, 2] if columns > 2 else [0]
    token_planes = [0, 1] if planes > 1 else [0]
    row_columns = list(range(0, columns, 4))
    row_planes = list(range(0, planes, 2))

    def swap(array, axis, mask):
        size = mesh.shape[axis]
        return lax.ppermute(array, axis, [(i, i ^ mask) for i in range(size)])

    def body(latent_cache, index_keys, query_latent, index_query, index_gates, selected):
        per, _, width = query_latent.shape
        heads = query_latent.shape[1]
        tokens = latent_cache.shape[0]
        runs = tokens // RUN
        all_runs = runs * columns * planes
        masked = all_runs != selected.shape[1]
        slab = jnp.swapaxes(latent_cache, 0, 1)
        query = jnp.swapaxes(query_latent, 1, 2)

        def after(array, *others):
            return lax.optimization_barrier((array, *others))[0]

        gate_rows = jnp.pad(
            index_gates[:, None, :], ((0, 0), (0, AUX - 1), (0, LANES - index_gates.shape[1]))
        )
        meta = jnp.concatenate([index_query, gate_rows], axis=1)
        meta = jnp.concatenate([meta, swap(meta, "ctx", 1)])

        packed = with_table(query, selected, all_runs // LANES)
        starts = {across: swap(packed, "row", across) if across else packed for across in row_planes}
        groups = {
            across: {mask: swap(start, "ctx", mask) if mask else start for mask in row_columns}
            for across, start in starts.items()
        }
        far_queries = [pack for group in groups.values() for pack in group.values()]
        half, quarter = tokens // 2, tokens // 4
        pieces, sent, shown = [(0, 0, slab)], [], []
        for across in token_planes[1:]:
            for offset, count in ((0, half), (half, quarter)):
                piece = slab[:, offset : offset + count]
                sent.append(swap(after(piece, *sent[-1:]), "row", across))
                pieces.append((across, offset, sent[-1]))
        slabs, places = [], []
        for across, offset, piece in pieces:
            for mask in token_columns:
                one = piece
                if mask:
                    late = list(starts.values()) if offset else []
                    one = swap(after(piece, *late, *shown[-1:]), "ctx", mask)
                    shown.append(one)
                for core in (0, 1):
                    if core and mask and offset:
                        one = after(one, *far_queries)
                    places.append((len(slabs), 0, piece.shape[1], core, across, mask, offset))
                    slabs.append(swap(one, "ctx", 1) if core else one)
        for across in token_planes[1:]:
            first = half + quarter
            both = [held[:, first:] for held in (slab, *shown[:1])]
            both = swap(jnp.concatenate(both, axis=1), "row", across)
            for core in (0, 1):
                for i, mask in enumerate(token_columns):
                    places.append((len(slabs), i * quarter, quarter, core, across, mask, first))
                slabs.append(swap(both, "ctx", 1) if core else both)

        masks = [0]
        for bit in [1 << k for k in range(2, columns.bit_length() - 1)] + token_columns[1:]:
            meta = after(meta, *(shown[-1:] if bit in token_columns else far_queries))
            meta = jnp.concatenate([meta, swap(meta, "ctx", bit)])
            masks += [mask ^ bit for mask in masks]

        parts, last = [], []
        split, halves = 2, []
        some = per // split
        for across in row_planes[1:] + row_planes[:1]:
            mine = []
            for mask in reversed(row_columns):
                pack = after(groups[across][mask], *last) if last else groups[across][mask]
                sizes = (planes, tokens)
                done = attend([pack], slabs, places, width, sizes, masked, split if across else 1)
                last = list(done)
                mine.append([swap(a, "ctx", mask) if mask else a for a in done] if across else done)
            if across:
                back = []
                for i in range(split):
                    rows = range(i * some, (i + 1) * some)
                    mixed = combine([part[i] for part in mine], [rows[0]] * len(mine), rows, heads)
                    back.append(swap(mixed, "row", across))
                    halves.append(mixed)
                    last = last + [mixed, meta] if i == 0 else last
                parts.append(back)
            else:
                waits = [back[0] for back in parts] + halves + [part[0] for part in mine]
                own = [
                    swap(after(part[0], *waits), "ctx", mask) if mask else part[0]
                    for mask, part in zip(reversed(row_columns), mine)
                ]
        index_scores = index_block(after(meta, *last), index_keys, index_query.shape[1], per, masks)
        attended = None
        for i in range(split):
            rows = range(i * some, (i + 1) * some)
            far = [back[i] for back in parts]
            begins = [rows[0]] * len(far) + [0] * len(own)
            cost = TINY if i == split - 1 else LONG
            attended = finish(far + own, begins, rows, per, heads, attended, cost)
        return attended, index_scores

    return jax.shard_map(
        body,
        mesh=mesh,
        in_specs=(
            P(("ctx", "row"), None),
            P("ctx", None),
            P(("row", "ctx"), None, None),
            P(("row", "ctx"), None, None),
            P(("row", "ctx"), None),
            P(("row", "ctx"), None),
        ),
        out_specs=(P(("row", "ctx"), None, None), P("row", "ctx")),
        check_vma=False,
    )
```
